512 devices in a mesh: dp: 64 (over y_lo, z, core), mp: 8 (over y_hi, x).
Axes of the slice: x: 4, y: 8 (y_hi: 2, y_lo: 4; y = y_hi * 4 + y_lo), z: 8, core: 2. Of those that a mesh axis runs over, the one named last changes fastest.
Arguments:
- tokens: bfloat16 [1024, 6144], P('dp', 'mp'), may hold values from -6 to 6
- norm_gain: float32 [6144], P('mp'), may hold values from 0.25 to 1.75
- w_up: bfloat16 [6144, 24576], P('mp', 'dp'), may hold values from -0.078125 to 0.078125
- cotangent: bfloat16 [1024, 24576], P('mp', 'dp'), may hold values from -32 to 32
Outputs:
- sharp_grad: float32 [6144, 24576], P('mp', 'dp')
The draws below stay inside these ranges and needn't reach their ends.
All inputs are finite; a program needn't handle non-finite values.
Results may differ from the reference program's by a relative error of at most 0.0048.
Values may be sent and summed in bfloat16 or wider, within the bound.
No kernel may reach another device: no remote copies, remote signals or barrier semaphores. Data moves between devices by JAX's collectives and lax.ppermute only.
A program may use at most 64 MiB of HBM per device.

```python
import math
import jax
import jax.numpy as jnp
from jax import lax

D = 6144
FF = 24576
TOKENS = 1024


def token_signs(key):
    key = jax.random.fold_in(key, 101)
    flips = jax.random.randint(key, (TOKENS, 1), 0, 2)
    return (2 * flips - 1).astype(jnp.float32)


def signed_profile(key, length, lower, upper):
    keys = jax.random.split(key, 2)
    magnitude = jax.random.uniform(keys[0], (1, length), jnp.float32, lower, upper)
    flips = jax.random.randint(keys[1], (1, length), 0, 2)
    return magnitude * (2 * flips - 1).astype(jnp.float32)


def window_mask(key, length, width):
    start = jax.random.randint(key, (), 0, length - width + 1)
    position = jnp.arange(length, dtype=jnp.int32)
    inside = (position >= start) & (position < start + width)
    return inside.astype(jnp.float32)[None, :]


def draw_tokens(key, part):
    signs = token_signs(key)
    key = jax.random.fold_in(key, 5)
    keys = jax.random.split(key, 3)
    profile = signed_profile(keys[0], D, 0.4, 1.0) * window_mask(keys[1], D, D // 8)
    base = jnp.clip(jax.random.normal(keys[2], (TOKENS, D), jnp.float32), -4.0, 4.0)
    return (base + signs * profile).astype(jnp.bfloat16)


def draw_cotangent(key, part):
    signs = token_signs(key)
    key = jax.random.fold_in(key, 7)
    keys = jax.random.split(key, 6)
    row_scale = jnp.exp(jax.random.uniform(keys[0], (TOKENS, 1), jnp.float32, math.log(0.3), math.log(3.0)))
    position = jnp.arange(FF, dtype=jnp.float32) / FF
    col_scale = jnp.exp(math.log(3.0) * position[None, :] + jax.random.uniform(keys[1], (1, FF), jnp.float32, -0.5, 0.5))
    coherent = signed_profile(keys[4], FF, 0.5, 1.2) * window_mask(keys[5], FF, FF // 16)
    base = jnp.clip(jax.random.normal(keys[2], (TOKENS, FF), jnp.float32), -4.0, 4.0)
    return (0.5 * base * row_scale * col_scale + signs * coherent).astype(jnp.bfloat16)


def level_of(rng, extent, shards, smallest, top_value):
    level = 1.0
    for dim, blocks in shards:
        heights = jax.random.uniform(jax.random.fold_in(jax.random.fold_in(rng, 6), dim), (blocks,), jnp.float32, smallest / len(shards), top_value / len(shards))
        level = level * jnp.repeat(jnp.exp(heights), extent[dim] // blocks).reshape((-1,) + (1,) * (len(extent) - 1 - dim))
    return level


def centred(rng, shape, deviation, bound, cuts=(), kind=jnp.bfloat16):
    entries = jax.random.normal(rng, shape, jnp.float32) * deviation
    if len(cuts) > 0:
        entries = level_of(rng, shape, cuts, -0.22, 0.18) * entries
    return jnp.clip(entries, min=-bound, max=bound).astype(kind)


def setup_inputs(seed: int = 0) -> dict:
    arg_keys = jax.random.split(jax.random.key(seed), 5)
    tokens = draw_tokens(jax.random.fold_in(arg_keys[4], 71), 0)
    norm_gain = jnp.clip(1.0 + 0.15 * jax.random.normal(arg_keys[1], (D,), jnp.float32), 0.25, 1.75)
    w_up = centred(arg_keys[2], (D, FF), D ** -0.5, 0.078125, ((0, 8), (1, 64)))
    cotangent = draw_cotangent(jax.random.fold_in(arg_keys[4], 71), 0)
    return {"tokens": tokens, "norm_gain": norm_gain, "w_up": w_up, "cotangent": cotangent}


def gelu_slope(value):
    cdf = 0.5 * (1.0 + lax.erf(value * (1.0 / math.sqrt(2.0))))
    dens = jnp.exp(-0.5 * value * value) * (1.0 / math.sqrt(2.0 * math.pi))
    return cdf + value * dens

def weight_grad(normed, weights, cotangent):
    pre = jnp.dot(normed, weights, preferred_element_type=jnp.float32)
    scale = 1.0 / math.sqrt(TOKENS)
    slope = (cotangent.astype(jnp.float32) * gelu_slope(pre) * scale).astype(jnp.bfloat16)
    return jnp.dot(normed.T, slope, preferred_element_type=jnp.float32)

def reference(tokens, norm_gain, w_up, cotangent):
    values = tokens.astype(jnp.float32)
    mean = lax.optimization_barrier(jnp.sum(values, axis=1)) / D
    var = lax.optimization_barrier(jnp.sum(values * values, axis=1)) / D - mean * mean
    normed = ((values - mean[:, None]) * lax.rsqrt(var[:, None] + 1e-06) * norm_gain[None, :]).astype(jnp.bfloat16)
    ascent = weight_grad(normed, w_up, cotangent)
    size = jnp.sqrt(jnp.sum(ascent * ascent)) + 1e-12
    radius = 0.5 * math.sqrt(FF)
    perturbed = (w_up.astype(jnp.float32) + radius * ascent / size).astype(jnp.bfloat16)
    return weight_grad(normed, perturbed, cotangent)
```

```python
import math

import jax
import jax.numpy as jnp
from jax import lax
from jax.sharding import Mesh
from jax.sharding import PartitionSpec as P

FF = 24576
D = 6144
TOKENS = 1024
DP = ("yl", "z", "c")
MP = ("yh", "x")
BF = jnp.bfloat16
F32 = jnp.float32


def gelu_slope(value):
    cdf = 0.5 * (1.0 + lax.erf(value * (1.0 / math.sqrt(2.0))))
    dens = jnp.exp(-0.5 * value * value) * (1.0 / math.sqrt(2.0 * math.pi))
    return cdf + value * dens


def swap(value, axis, bit):
    size = lax.axis_size(axis)
    return lax.ppermute(value, axis, [(i, i ^ bit) for i in range(size)])


def butterfly(value, steps):
    for axis, bit in steps:
        value = value + swap(value, axis, bit)
    return value


OVER_MP = (("x", 1), ("x", 2), ("yh", 1))
OVER_DP = (("c", 1), ("z", 1), ("z", 2), ("z", 4), ("yl", 1), ("yl", 2))


def spread(value, axes, count):
    copies = jnp.broadcast_to(value[None], (count,) + value.shape)
    return lax.all_to_all(copies, axes, 0, 0, tiled=True)


def spread_dp(value):
    mine = spread(value, ("yl", "z"), 32)
    other = swap(mine, "c", 1)
    core = lax.axis_index("c")
    first = jnp.where(core == 0, mine, other)
    second = jnp.where(core == 0, other, mine)
    return jnp.stack([first, second], axis=1)


def per_device(tokens, norm_gain, w_up, cotangent):
    scale = 1.0 / math.sqrt(TOKENS)
    with jax.named_scope("token_gather"):
        raw = spread_dp(tokens).reshape(TOKENS, -1)
    with jax.named_scope("stats"):
        values = tokens.astype(F32)
        sums = jnp.stack([jnp.sum(values, axis=1), jnp.sum(values * values, axis=1)])
        sums = butterfly(sums, OVER_MP)
        place = lax.axis_index(DP)
        mine = (jnp.arange(64) == place)[None, :, None]
        sums = jnp.where(mine, sums[:, None, :], 0.0).reshape(16, 128)
        sums = butterfly(sums, OVER_DP).reshape(2, TOKENS)
        mean = sums[0] / D
        var = sums[1] / D - mean * mean
        inv = lax.rsqrt(var + 1e-06)
    with jax.named_scope("cot_gather"):
        cot = spread(cotangent, MP, 8).reshape(TOKENS, -1)
    with jax.named_scope("normalize"):
        normed = ((raw.astype(F32) - mean[:, None]) * inv[:, None] * norm_gain[None, :]).astype(BF)
    with jax.named_scope("gram"):
        rows = lax.dynamic_slice_in_dim(normed, place * 16, 16, 0)
        gram = lax.dot_general(rows, normed, (((1,), (1,)), ((), ())), preferred_element_type=F32)
        gram = spread(gram.astype(BF), MP, 8)
        gram = jnp.sum(gram.astype(F32), axis=0).astype(BF)
        gram = spread_dp(gram).reshape(TOKENS, TOKENS)
    with jax.named_scope("project"):
        part = jnp.dot(normed, w_up, preferred_element_type=F32).astype(BF)
        part = lax.all_to_all(part.reshape(8, 128, -1), MP, 0, 0, tiled=True)
        own = jnp.sum(part.astype(F32), axis=0).astype(BF)
        pre = spread(own, MP, 8).reshape(TOKENS, -1).astype(F32)

    def slope_at(value):
        return (cot.astype(F32) * gelu_slope(value) * scale).astype(BF)

    with jax.named_scope("ascent"):
        slope = slope_at(pre)
        along = jnp.dot(gram, slope, preferred_element_type=F32)
        squared = jnp.sum(slope.astype(F32) * along)
        squared = butterfly(squared.reshape(1, 1), OVER_DP)
        size = jnp.sqrt(jnp.maximum(squared, 0.0)) + 1e-12
        radius = 0.5 * math.sqrt(FF)
    with jax.named_scope("sharp"):
        sharp = slope_at(pre + along * (radius / size))
        return lax.dot_general(normed, sharp, (((0,), (0,)), ((), ())), preferred_element_type=F32)


def solution(mesh):
    fine = Mesh(mesh.devices.reshape(4, 8, 2, 2, 4), DP + MP)
    placed = (P(DP, MP), P(MP), P(MP, DP), P(MP, DP))
    return jax.shard_map(
        per_device, mesh=fine, in_specs=placed, out_specs=P(MP, DP), check_vma=False
    )
```

```python
import math

import jax
import jax.numpy as jnp
from jax import lax
from jax.sharding import Mesh
from jax.sharding import PartitionSpec as P

FF = 24576
D = 6144
TOKENS = 1024
DP = ("yl", "z", "c")
MP = ("yh", "x")
BF = jnp.bfloat16
F32 = jnp.float32


def gelu_slope(value):
    cdf = 0.5 * (1.0 + lax.erf(value * (1.0 / math.sqrt(2.0))))
    dens = jnp.exp(-0.5 * value * value) * (1.0 / math.sqrt(2.0 * math.pi))
    return cdf + value * dens


def swap(value, axis, bit):
    size = lax.axis_size(axis)
    return lax.ppermute(value, axis, [(i, i ^ bit) for i in range(size)])


def spread(value, axes, count):
    copies = jnp.broadcast_to(value[None], (count,) + value.shape)
    return lax.all_to_all(copies, axes, 0, 0, tiled=True)


def spread_dp(value):
    mine = spread(value, ("yl", "z"), 32)
    other = swap(mine, "c", 1)
    core = lax.axis_index("c")
    first = jnp.where(core == 0, mine, other)
    second = jnp.where(core == 0, other, mine)
    return jnp.stack([first, second], axis=1)


def ordered(blocks, index):
    odd, high = (index & 1) == 1, (index & 2) == 2
    near = [jnp.where(odd, blocks[q ^ 1], blocks[q]) for q in range(4)]
    return [jnp.where(high, near[q ^ 2], near[q]) for q in range(4)]


def gather_x(value):
    x = lax.axis_index("x")
    blocks = [value] + [swap(value, "x", b) for b in (1, 2, 3)]
    return ordered(blocks, x)


def pair_y(value):
    other = swap(value, "yh", 1)
    low = lax.axis_index("yh") == 0
    return jnp.stack([jnp.where(low, value, other), jnp.where(low, other, value)])


def per_device(tokens, norm_gain, w_up, cotangent):
    scale = 1.0 / math.sqrt(TOKENS)
    columns = w_up.shape[1]
    x = lax.axis_index("x")
    with jax.named_scope("stats"):
        values = tokens.astype(F32)
        sums = jnp.stack([jnp.sum(values, axis=1), jnp.sum(values * values, axis=1)])
        for axis, bit in (("x", 1), ("x", 2), ("yh", 1)):
            sums = sums + swap(sums, axis, bit)
        mean = sums[0] / D
        var = sums[1] / D - mean * mean
        inv = lax.rsqrt(var + 1e-06)
        rows = ((values - mean[:, None]) * inv[:, None] * norm_gain[None, :]).astype(BF)
    with jax.named_scope("token_gather"):
        normed = spread_dp(rows).reshape(TOKENS, -1)
    with jax.named_scope("cot_gather"):
        cot = jnp.stack(gather_x(pair_y(cotangent)), axis=1).reshape(TOKENS, columns)
    with jax.named_scope("gram"):
        gram = lax.dot_general(rows, normed, (((1,), (1,)), ((), ())), preferred_element_type=F32)
        gram = spread(gram.astype(BF), MP, 8)
        gram = jnp.sum(gram.astype(F32), axis=0).astype(BF)
        gram = spread_dp(gram).reshape(TOKENS, TOKENS)
    with jax.named_scope("project"):
        part = jnp.dot(normed, w_up, preferred_element_type=F32).astype(BF)
        part = part.reshape(4, 256, columns)

        def block(b):
            return lax.dynamic_index_in_dim(part, x ^ b, 0, keepdims=False)

        total = block(0).astype(F32)
        for b in (1, 2, 3):
            total = total + swap(block(b), "x", b).astype(F32)
        half = total.astype(BF)
        both = (half.astype(F32) + swap(half, "yh", 1).astype(F32)).astype(BF)
        pre = jnp.concatenate(gather_x(both), axis=0).astype(F32)

    def slope_at(value):
        return (cot.astype(F32) * gelu_slope(value) * scale).astype(BF)

    with jax.named_scope("ascent"):
        slope = slope_at(pre)
        along = jnp.dot(gram, slope, preferred_element_type=F32)
        squared = jnp.sum(slope.astype(F32) * along)
        squared = jnp.sum(spread(jnp.full((1, 128), squared), DP, 64)[:, 0, 0])
        size = jnp.sqrt(jnp.maximum(squared, 0.0)) + 1e-12
        radius = 0.5 * math.sqrt(FF)
    with jax.named_scope("sharp"):
        sharp = slope_at(pre + along * (radius / size))
        return lax.dot_general(normed, sharp, (((0,), (0,)), ((), ())), preferred_element_type=F32)


def solution(mesh):
    fine = Mesh(mesh.devices.reshape(4, 8, 2, 2, 4), DP + MP)
    placed = (P(DP, MP), P(MP), P(MP, DP), P(MP, DP))
    return jax.shard_map(
        per_device, mesh=fine, in_specs=placed, out_specs=P(MP, DP), check_vma=False
    )
```

```python
import math

import jax
import jax.numpy as jnp
from jax import lax
from jax.sharding import Mesh
from jax.sharding import PartitionSpec as P

FF = 24576
D = 6144
TOKENS = 1024
DP = ("yl", "z", "c")
MP = ("yh", "x")
BF = jnp.bfloat16
F32 = jnp.float32


def gelu_slope(value):
    cdf = 0.5 * (1.0 + lax.erf(value * (1.0 / math.sqrt(2.0))))
    dens = jnp.exp(-0.5 * value * value) * (1.0 / math.sqrt(2.0 * math.pi))
    return cdf + value * dens


def swap(value, axis, bit):
    size = lax.axis_size(axis)
    return lax.ppermute(value, axis, [(i, i ^ bit) for i in range(size)])


def spread(value, axes, count):
    copies = jnp.broadcast_to(value[None], (count,) + value.shape)
    return lax.all_to_all(copies, axes, 0, 0, tiled=True)


def spread_dp(value):
    mine = spread(value, ("yl", "z"), 32)
    other = swap(mine, "c", 1)
    core = lax.axis_index("c")
    first = jnp.where(core == 0, mine, other)
    second = jnp.where(core == 0, other, mine)
    return jnp.stack([first, second], axis=1)


def ordered(blocks, index):
    odd, high = (index & 1) == 1, (index & 2) == 2
    near = [jnp.where(odd, blocks[q ^ 1], blocks[q]) for q in range(4)]
    return [jnp.where(high, near[q ^ 2], near[q]) for q in range(4)]


def gather_x(value):
    x = lax.axis_index("x")
    blocks = [value] + [swap(value, "x", b) for b in (1, 2, 3)]
    return ordered(blocks, x)


def pair_y(value):
    other = swap(value, "yh", 1)
    low = lax.axis_index("yh") == 0
    return jnp.stack([jnp.where(low, value, other), jnp.where(low, other, value)])


def after(value, *others):
    return lax.optimization_barrier((value,) + others)[0]


def rounded(value):
    return lax.reduce_precision(value, 8, 7)


def terms(value, count):
    out = []
    for _ in range(count):
        out.append(rounded(value))
        value = value - out[-1]
    return out


def dot(left, right, dims, precision=None):
    return lax.dot_general(left, right, (dims, ((), ())), precision=precision, preferred_element_type=F32)


def per_device(tokens, norm_gain, w_up, cotangent):
    scale = 1.0 / math.sqrt(TOKENS)
    width, columns = w_up.shape
    x = lax.axis_index("x")
    place = lax.axis_index(DP)
    exact = lax.Precision.HIGHEST
    with jax.named_scope("token_gather"):
        raw = spread(tokens, ("yl", "z"), 32)
    with jax.named_scope("cot_gather"):
        cot = gather_x(pair_y(cotangent))
        cot = jnp.stack(cot, axis=1).reshape(TOKENS, columns)
    with jax.named_scope("token_swap"):
        raw = after(raw, cot)
        other = swap(raw, "c", 1)
        even = lax.axis_index("c") == 0
        raw = jnp.stack([jnp.where(even, raw, other), jnp.where(even, other, raw)], axis=1)
        values = raw.reshape(TOKENS, width).astype(F32)
    with jax.named_scope("local_stats"):
        local = jnp.sum(values, axis=1) / width
        centred = values - local[:, None]
        css = jnp.sum(centred * centred, axis=1)
        full = centred * norm_gain[None, :]
        high = rounded(full)
        low = (full - high).astype(BF)
        high = high.astype(BF)
        lean = jnp.sum(high.astype(F32) * norm_gain[None, :], axis=1)
        power = jnp.sum(norm_gain * norm_gain)
        column = jnp.sum(w_up.astype(F32) * norm_gain[:, None], axis=0)
    with jax.named_scope("gram_part"):
        gram = dot(lax.dynamic_slice_in_dim(high, place * 16, 16, 0), high, ((1,), (1,)))
        c1, c2 = terms(column, 2)
        b1, b2 = terms(power, 2)
        pad = jnp.zeros((TOKENS - 2 * columns - 2,), F32)
        extra = jnp.concatenate([c1, c2, b1[None], b2[None], pad])
        sent = jnp.stack(terms(local, 3) + terms(css, 2) + terms(lean, 2) + [extra])
        sent = jnp.concatenate([gram, sent], axis=0).astype(BF)
        got = spread(sent, MP, 8).astype(F32)
    with jax.named_scope("project"):
        part = dot(high, w_up, ((1,), (0,))) + dot(low, w_up, ((1,), (0,)))
        part = part.astype(BF).reshape(4, 256, columns)

        def block(b):
            return lax.dynamic_index_in_dim(part, x ^ b, 0, keepdims=False)

        total = block(0).astype(F32)
        for b in (1, 2, 3):
            total = total + swap(block(b), "x", b).astype(F32)
        total = total + swap(total.astype(BF), "yh", 1).astype(F32)
    with jax.named_scope("stats"):
        local = got[:, 16] + got[:, 17] + got[:, 18]
        css = got[:, 19] + got[:, 20]
        lean = got[:, 21] + got[:, 22]
        column = got[:, 23, :columns] + got[:, 23, columns : 2 * columns]
        power = got[:, 23, 2 * columns : 2 * columns + 1] + got[:, 23, 2 * columns + 1 : 2 * columns + 2]
        mean = jnp.sum(local, axis=0) / 8
        apart = local - mean[None, :]
        var = (jnp.sum(css, axis=0) + width * jnp.sum(apart * apart, axis=0)) / D
        inv = lax.rsqrt(var + 1e-06)
        normed = ((values - mean[:, None]) * inv[:, None] * norm_gain[None, :]).astype(BF)
    with jax.named_scope("gram"):
        left = jnp.concatenate([lean, apart, power * apart], axis=0) * inv[None, :]
        left = lax.dynamic_slice_in_dim(left, place * 16, 16, 1)
        mine = lax.dynamic_slice_in_dim(inv, place * 16, 16, 0)
        right = jnp.concatenate([apart, lean, apart], axis=0)
        rows = jnp.sum(got[:, :16], axis=0) * mine[:, None] + dot(left, right, ((0,), (0,)), exact)
        gram = spread_dp((rows * inv[None, :]).astype(BF)).reshape(TOKENS, TOKENS)
    with jax.named_scope("pre"):
        shift = dot(lax.dynamic_slice_in_dim(apart, x * 256, 256, 1), column, ((0,), (0,)), exact)
        total = (total + shift) * lax.dynamic_slice_in_dim(inv, x * 256, 256, 0)[:, None]
        pre = jnp.concatenate(gather_x(total.astype(BF)), axis=0).astype(F32)

    def slope_at(value):
        return (cot.astype(F32) * gelu_slope(value) * scale).astype(BF)

    with jax.named_scope("ascent"):
        slope = slope_at(pre)
        along = dot(gram, slope, ((1,), (0,)))
        squared = jnp.sum(slope.astype(F32) * along)
        squared = jnp.sum(spread(jnp.full((1, 128), squared), DP, 64)[:, 0, 0])
        size = jnp.sqrt(jnp.maximum(squared, 0.0)) + 1e-12
        radius = 0.5 * math.sqrt(FF)
    with jax.named_scope("sharp"):
        sharp = slope_at(pre + along * (radius / size))
        return dot(normed, sharp, ((0,), (0,)))


def solution(mesh):
    fine = Mesh(mesh.devices.reshape(4, 8, 2, 2, 4), DP + MP)
    placed = (P(DP, MP), P(MP), P(MP, DP), P(MP, DP))
    return jax.shard_map(
        per_device, mesh=fine, in_specs=placed, out_specs=P(MP, DP), check_vma=False
    )
```

```python
import math

import jax
import jax.numpy as jnp
from jax import lax
from jax.sharding import Mesh
from jax.sharding import PartitionSpec as P

FF = 24576
D = 6144
TOKENS = 1024
DP = ("yl", "z", "c")
MP = ("yh", "x")
BF = jnp.bfloat16
F32 = jnp.float32


def gelu_slope(value):
    cdf = 0.5 * (1.0 + lax.erf(value * (1.0 / math.sqrt(2.0))))
    dens = jnp.exp(-0.5 * value * value) * (1.0 / math.sqrt(2.0 * math.pi))
    return cdf + value * dens


def swap(value, axis, bit):
    size = lax.axis_size(axis)
    return lax.ppermute(value, axis, [(i, i ^ bit) for i in range(size)])


def spread(value, axes, count):
    copies = jnp.broadcast_to(value[None], (count,) + value.shape)
    return lax.all_to_all(copies, axes, 0, 0, tiled=True)


def after(value, *others):
    return lax.optimization_barrier((value,) + others)[0]


def join_cores(mine):
    other = swap(mine, "c", 1)
    even = lax.axis_index("c") == 0
    return jnp.stack([jnp.where(even, mine, other), jnp.where(even, other, mine)], axis=1)


def ordered(blocks, index):
    odd, high = (index & 1) == 1, (index & 2) == 2
    near = [jnp.where(odd, blocks[q ^ 1], blocks[q]) for q in range(4)]
    return [jnp.where(high, near[q ^ 2], near[q]) for q in range(4)]


def gather_x(value):
    return [value] + [swap(value, "x", b) for b in (1, 2, 3)]


def pair_y(value):
    other = swap(value, "yh", 1)
    low = lax.axis_index("yh") == 0
    return jnp.stack([jnp.where(low, value, other), jnp.where(low, other, value)])


def dot(left, right, dims):
    return lax.dot_general(left, right, (dims, ((), ())), preferred_element_type=F32)


def per_device(tokens, norm_gain, w_up, cotangent):
    scale = 1.0 / math.sqrt(TOKENS)
    columns = w_up.shape[1]
    x = lax.axis_index("x")
    with jax.named_scope("stats"):
        values = tokens.astype(F32)
        sums = jnp.concatenate([jnp.sum(values, axis=1), jnp.sum(values * values, axis=1)])
        sums = spread(sums[None], MP, 8)
        pair = pair_y(cotangent)
        sums = jnp.sum(after(sums, pair), axis=(0, 1))
        mean = sums[:16] / D
        var = sums[16:] / D - mean * mean
        inv = lax.rsqrt(var + 1e-06)
        rows = ((values - mean[:, None]) * inv[:, None] * norm_gain[None, :]).astype(BF)
    with jax.named_scope("token_gather"):
        mine = spread(rows, ("yl", "z"), 32)
        cot = gather_x(after(pair, rows))
        normed = join_cores(after(mine, *cot)).reshape(TOKENS, -1)
        cot = jnp.stack(ordered(cot, x), axis=1).reshape(TOKENS, columns)
    with jax.named_scope("gram_part"):
        gram = dot(rows, normed, ((1,), (1,)))
        gram = spread(gram.astype(BF), MP, 8)
    with jax.named_scope("project"):
        part = dot(normed, w_up, ((1,), (0,))).astype(BF).reshape(4, 256, columns)

        def block(b):
            return lax.dynamic_index_in_dim(part, x ^ b, 0, keepdims=False)

        moved = [swap(block(b), "x", b) for b in (1, 2, 3)]
        gram = after(gram, *moved)
        total = block(0).astype(F32) + sum(m.astype(F32) for m in moved)
    with jax.named_scope("gram_gather"):
        gram = jnp.sum(gram.astype(F32), axis=0).astype(BF)
        gram = spread(gram, ("yl", "z"), 32)
    with jax.named_scope("pre"):
        total = total + swap(total.astype(BF), "yh", 1).astype(F32)
        moved = gather_x(total.astype(BF))
        gram = join_cores(after(gram, *moved)).reshape(TOKENS, TOKENS)
        pre = jnp.concatenate(ordered(moved, x), axis=0).astype(F32)

    def slope_at(value):
        return (cot.astype(F32) * gelu_slope(value) * scale).astype(BF)

    with jax.named_scope("ascent"):
        slope = slope_at(pre)
        along = dot(gram, slope, ((1,), (0,)))
        squared = jnp.sum(slope.astype(F32) * along)
        squared = jnp.sum(spread(jnp.full((1, 128), squared), DP, 64)[:, 0, 0])
        size = jnp.sqrt(jnp.maximum(squared, 0.0)) + 1e-12
        radius = 0.5 * math.sqrt(FF)
    with jax.named_scope("sharp"):
        sharp = slope_at(pre + along * (radius / size))
        return dot(normed, sharp, ((0,), (0,)))


def solution(mesh):
    fine = Mesh(mesh.devices.reshape(4, 8, 2, 2, 4), DP + MP)
    placed = (P(DP, MP), P(MP), P(MP, DP), P(MP, DP))
    return jax.shard_map(
        per_device, mesh=fine, in_specs=placed, out_specs=P(MP, DP), check_vma=False
    )
```

```python
import math

import jax
import jax.numpy as jnp
from jax import lax
from jax.experimental import pallas as pl
from jax.experimental.pallas import tpu as pltpu
from jax.sharding import Mesh
from jax.sharding import PartitionSpec as P

FF = 24576
D = 6144
TOKENS = 1024
DP = ("yl", "z", "c")
MP = ("yh", "x")
BF = jnp.bfloat16
F32 = jnp.float32


def gelu_slope(value):
    cdf = 0.5 * (1.0 + lax.erf(value * (1.0 / math.sqrt(2.0))))
    dens = jnp.exp(-0.5 * value * value) * (1.0 / math.sqrt(2.0 * math.pi))
    return cdf + value * dens


def swap(value, axis, bit):
    size = lax.axis_size(axis)
    return lax.ppermute(value, axis, [(i, i ^ bit) for i in range(size)])


def spread(value, axes, count):
    copies = jnp.broadcast_to(value[None], (count,) + value.shape)
    return lax.all_to_all(copies, axes, 0, 0, tiled=True)


def after(value, *others):
    return lax.optimization_barrier((value,) + others)[0]


def join_cores(mine):
    other = swap(mine, "c", 1)
    even = lax.axis_index("c") == 0
    return jnp.stack([jnp.where(even, mine, other), jnp.where(even, other, mine)], axis=1)


def ordered(blocks, index):
    odd, high = (index & 1) == 1, (index & 2) == 2
    near = [jnp.where(odd, blocks[q ^ 1], blocks[q]) for q in range(4)]
    return [jnp.where(high, near[q ^ 2], near[q]) for q in range(4)]


def gather_x(value):
    return [value] + [swap(value, "x", b) for b in (1, 2, 3)]


def pair_y(value):
    other = swap(value, "yh", 1)
    low = lax.axis_index("yh") == 0
    return jnp.stack([jnp.where(low, value, other), jnp.where(low, other, value)])


def dot(left, right, dims, precision=None):
    return lax.dot_general(left, right, (dims, ((), ())), precision=precision, preferred_element_type=F32)


def split(value, count):
    out = []
    for _ in range(count):
        out.append(value.astype(BF).astype(F32))
        value = value - out[-1]
    return out


def local_kernel(at, mine, other, gain, w, joined, own, near, opposite, far, sent, high, part):
    place, core, x = at[0], at[1], at[2]
    g = gain[...]
    width = g.shape[1]
    ones = jnp.ones((8, width), BF)
    gains = jnp.concatenate(split(g, 3) + [jnp.zeros((5, width), F32)], axis=0).astype(BF)
    local, css, lean = [], [], []
    for i in range(8):
        chips = pl.ds(4 * i, 4)
        joined[chips, core] = mine[chips]
        joined[chips, 1 - core] = other[chips]
        raw = joined[chips].reshape(128, width)
        value = raw.astype(F32)
        centred = value - jnp.sum(value, axis=1, keepdims=True) * (1.0 / width)
        full = centred * g
        first = full.astype(BF)
        second = (full - first.astype(F32)).astype(BF)
        high[pl.ds(128 * i, 128)] = first
        rows = dot(first, w[...], ((1,), (0,))) + dot(second, w[...], ((1,), (0,)))
        part[i // 2, pl.ds(128 * (i % 2), 128)] = rows
        square = centred * centred
        top = square.astype(BF)
        rest = (square - top.astype(F32)).astype(BF)
        across = ((1,), (1,))
        local.append(dot(ones, raw, across)[:1] * (1.0 / width))
        css.append((dot(ones, top, across) + dot(ones, rest, across))[:1])
        lean.append(jnp.sum(dot(gains, first, across), axis=0, keepdims=True))
    own[...] = part[x]
    near[...] = part[x ^ 1].astype(BF)
    opposite[...] = part[x ^ 2].astype(BF)
    far[...] = part[x ^ 3].astype(BF)
    gram = dot(high[pl.ds(pl.multiple_of(place * 16, 16), 16)], high[...], ((1,), (1,)))
    local, css, lean = (jnp.concatenate(v, axis=1) for v in (local, css, lean))
    column = jnp.sum(dot(gains, w[...], ((1,), (0,))), axis=0, keepdims=True)
    power = jnp.broadcast_to(jnp.sum(g * g, axis=1, keepdims=True), (1, 128))
    extra = jnp.concatenate(split(column, 2) + split(power, 2), axis=1)
    rows = [gram] + split(local, 3) + split(css, 2) + split(lean, 2) + [extra, jnp.zeros((8, TOKENS), F32)]
    sent[...] = jnp.concatenate(rows, axis=0).astype(BF)


def local_work(at, mine, other, gain, w):
    width, columns = w.shape
    block = jax.ShapeDtypeStruct((256, columns), BF)
    vmem = pl.BlockSpec(memory_space=pltpu.VMEM)
    return pl.pallas_call(
        local_kernel,
        out_shape=[
            jax.ShapeDtypeStruct((32, 2, 16, width), BF),
            jax.ShapeDtypeStruct((256, columns), F32),
            block,
            block,
            block,
            jax.ShapeDtypeStruct((32, TOKENS), BF),
        ],
        in_specs=[pl.BlockSpec(memory_space=pltpu.SMEM)] + [vmem] * 4,
        out_specs=[vmem] * 6,
        scratch_shapes=[pltpu.VMEM((TOKENS, width), BF), pltpu.VMEM((4, 256, columns), F32)],
        compiler_params=pltpu.CompilerParams(vmem_limit_bytes=40 << 20),
        cost_estimate=pl.CostEstimate(flops=2 * TOKENS * width * columns * 2, bytes_accessed=8 << 20, transcendentals=0),
        name="local_work",
    )(at, mine, other, gain, w)


def per_device(tokens, norm_gain, w_up, cotangent):
    scale = 1.0 / math.sqrt(TOKENS)
    width, columns = w_up.shape
    x = lax.axis_index("x")
    place = lax.axis_index(DP)
    exact = lax.Precision.HIGHEST
    with jax.named_scope("token_gather"):
        mine = spread(tokens, ("yl", "z"), 32)
        other = swap(mine, "c", 1)
    with jax.named_scope("local_work"):
        at = jnp.stack([place, lax.axis_index("c"), x]).astype(jnp.int32)
        joined, total, near, opposite, far, sent = local_work(at, mine, other, norm_gain[None], w_up)
    with jax.named_scope("sums_x"):
        got = spread(sent, MP, 8)
        moved = [swap(v, "x", b) for b, v in ((1, near), (2, opposite), (3, far))]
        pair = pair_y(after(cotangent, near))
        got = after(got, pair, *moved).astype(F32)
        total = total + sum(m.astype(F32) for m in moved)
    with jax.named_scope("stats"):
        local = got[:, 16] + got[:, 17] + got[:, 18]
        css = got[:, 19] + got[:, 20]
        lean = got[:, 21] + got[:, 22]
        column = got[:, 23, :columns] + got[:, 23, columns : 2 * columns]
        power = got[:, 23, 2 * columns : 2 * columns + 1] + got[:, 23, 2 * columns + 128 : 2 * columns + 129]
        mean = jnp.sum(local, axis=0) / 8
        apart = local - mean[None, :]
        var = (jnp.sum(css, axis=0) + width * jnp.sum(apart * apart, axis=0)) / D
        inv = lax.rsqrt(var + 1e-06)
    with jax.named_scope("gram"):
        left = jnp.concatenate([lean, apart, power * apart], axis=0) * inv[None, :]
        left = lax.dynamic_slice_in_dim(left, place * 16, 16, 1)
        own = lax.dynamic_slice_in_dim(inv, place * 16, 16, 0)
        right = jnp.concatenate([apart, lean, apart], axis=0)
        rows = jnp.sum(got[:, :16], axis=0) * own[:, None] + dot(left, right, ((0,), (0,)), exact)
        gram = spread((rows * inv[None, :]).astype(BF), ("yl", "z"), 32)
    with jax.named_scope("pre"):
        half = total.astype(BF)
        moved = swap(half, "yh", 1)
        cot = gather_x(after(pair, half))
        normed = joined.reshape(TOKENS, width).astype(F32) - mean[:, None]
        normed = (normed * inv[:, None] * norm_gain[None, :]).astype(BF)
        shift = dot(lax.dynamic_slice_in_dim(apart, x * 256, 256, 1), column, ((0,), (0,)), exact)
        total = total + shift
        total = (total + after(moved, normed, *cot).astype(F32)) * lax.dynamic_slice_in_dim(inv, x * 256, 256, 0)[:, None]
        moved = gather_x(total.astype(BF))
        cot = jnp.stack(ordered(cot, x), axis=1).reshape(TOKENS, columns)
        gram = join_cores(after(gram, cot, *moved)).reshape(TOKENS, TOKENS)
        pre = jnp.concatenate(ordered(moved, x), axis=0).astype(F32)

    def slope_at(value):
        return (cot.astype(F32) * gelu_slope(value) * scale).astype(BF)

    with jax.named_scope("ascent"):
        slope = slope_at(pre)
        along = dot(gram, slope, ((1,), (0,)))
        squared = jnp.sum(slope.astype(F32) * along)
        squared = jnp.sum(spread(jnp.full((1, 128), squared), DP, 64)[:, 0, 0])
        size = jnp.sqrt(jnp.maximum(squared, 0.0)) + 1e-12
        radius = 0.5 * math.sqrt(FF)
    with jax.named_scope("sharp"):
        sharp = slope_at(pre + along * (radius / size))
        return dot(normed, sharp, ((0,), (0,)))


def solution(mesh):
    fine = Mesh(mesh.devices.reshape(4, 8, 2, 2, 4), DP + MP)
    placed = (P(DP, MP), P(MP), P(MP, DP), P(MP, DP))
    return jax.shard_map(
        per_device, mesh=fine, in_specs=placed, out_specs=P(MP, DP), check_vma=False
    )
```

```python
import math

import jax
import jax.numpy as jnp
from jax import lax
from jax.experimental import pallas as pl
from jax.experimental.pallas import tpu as pltpu
from jax.sharding import Mesh
from jax.sharding import PartitionSpec as P

FF = 24576
D = 6144
TOKENS = 1024
DP = ("yl", "z", "c")
MP = ("yh", "x")
BF = jnp.bfloat16
F32 = jnp.float32


def gelu_slope(value):
    cdf = 0.5 * (1.0 + lax.erf(value * (1.0 / math.sqrt(2.0))))
    dens = jnp.exp(-0.5 * value * value) * (1.0 / math.sqrt(2.0 * math.pi))
    return cdf + value * dens


def swap(value, axis, bit):
    size = lax.axis_size(axis)
    return lax.ppermute(value, axis, [(i, i ^ bit) for i in range(size)])


def spread(value, axes, count):
    copies = jnp.broadcast_to(value[None], (count,) + value.shape)
    return lax.all_to_all(copies, axes, 0, 0, tiled=True)


def after(value, *others):
    return lax.optimization_barrier((value,) + others)[0]


def join_cores(mine):
    other = swap(mine, "c", 1)
    even = lax.axis_index("c") == 0
    return jnp.stack([jnp.where(even, mine, other), jnp.where(even, other, mine)], axis=1)


def ordered(blocks, index):
    odd, high = (index & 1) == 1, (index & 2) == 2
    near = [jnp.where(odd, blocks[q ^ 1], blocks[q]) for q in range(4)]
    return [jnp.where(high, near[q ^ 2], near[q]) for q in range(4)]


def gather_x(value):
    return [value] + [swap(value, "x", b) for b in (1, 2, 3)]


def pair_y(value):
    other = swap(value, "yh", 1)
    low = lax.axis_index("yh") == 0
    return jnp.stack([jnp.where(low, value, other), jnp.where(low, other, value)])


def dot(left, right, dims, precision=None):
    return lax.dot_general(left, right, (dims, ((), ())), precision=precision, preferred_element_type=F32)


def split(value, count):
    out = []
    for _ in range(count):
        out.append(value.astype(BF).astype(F32))
        value = value - out[-1]
    return out


def local_kernel(at, mine, other, gain, w, joined, own, near, opposite, far, sent, high, part):
    place, core, x = at[0], at[1], at[2]
    g = gain[...]
    width = g.shape[1]
    ones = jnp.ones((8, width), BF)
    gains = jnp.concatenate(split(g, 3) + [jnp.zeros((5, width), F32)], axis=0).astype(BF)
    local, css, lean = [], [], []
    for i in range(8):
        chips = pl.ds(4 * i, 4)
        joined[chips, core] = mine[chips]
        joined[chips, 1 - core] = other[chips]
        raw = joined[chips].reshape(128, width)
        value = raw.astype(F32)
        centred = value - jnp.sum(value, axis=1, keepdims=True) * (1.0 / width)
        full = centred * g
        first = full.astype(BF)
        second = (full - first.astype(F32)).astype(BF)
        high[pl.ds(128 * i, 128)] = first
        rows = dot(first, w[...], ((1,), (0,))) + dot(second, w[...], ((1,), (0,)))
        part[i // 2, pl.ds(128 * (i % 2), 128)] = rows
        square = centred * centred
        top = square.astype(BF)
        rest = (square - top.astype(F32)).astype(BF)
        across = ((1,), (1,))
        local.append(dot(ones, raw, across)[:1] * (1.0 / width))
        css.append((dot(ones, top, across) + dot(ones, rest, across))[:1])
        lean.append(jnp.sum(dot(gains, first, across), axis=0, keepdims=True))
    own[...] = part[x]
    near[...] = part[x ^ 1].astype(BF)
    opposite[...] = part[x ^ 2].astype(BF)
    far[...] = part[x ^ 3].astype(BF)
    gram = dot(high[pl.ds(pl.multiple_of(place * 16, 16), 16)], high[...], ((1,), (1,)))
    local, css, lean = (jnp.concatenate(v, axis=1) for v in (local, css, lean))
    column = jnp.sum(dot(gains, w[...], ((1,), (0,))), axis=0, keepdims=True)
    power = jnp.broadcast_to(jnp.sum(g * g, axis=1, keepdims=True), (1, 128))
    extra = jnp.concatenate(split(column, 2) + split(power, 2), axis=1)
    rows = [gram] + split(local, 3) + split(css, 2) + split(lean, 2) + [extra]
    sent[...] = jnp.concatenate(rows, axis=0).astype(BF)


def local_work(at, mine, other, gain, w):
    width, columns = w.shape
    block = jax.ShapeDtypeStruct((256, columns), BF)
    vmem = pl.BlockSpec(memory_space=pltpu.VMEM)
    return pl.pallas_call(
        local_kernel,
        out_shape=[
            jax.ShapeDtypeStruct((32, 2, 16, width), BF),
            jax.ShapeDtypeStruct((256, columns), F32),
            block,
            block,
            block,
            jax.ShapeDtypeStruct((24, TOKENS), BF),
        ],
        in_specs=[pl.BlockSpec(memory_space=pltpu.SMEM)] + [vmem] * 4,
        out_specs=[vmem] * 2 + [pl.BlockSpec()] * 4,
        scratch_shapes=[pltpu.VMEM((TOKENS, width), BF), pltpu.VMEM((4, 256, columns), F32)],
        compiler_params=pltpu.CompilerParams(vmem_limit_bytes=40 << 20),
        cost_estimate=pl.CostEstimate(flops=2 * TOKENS * width * columns * 2, bytes_accessed=8 << 20, transcendentals=0),
        name="local_work",
    )(at, mine, other, gain, w)


def per_device(tokens, norm_gain, w_up, cotangent):
    scale = 1.0 / math.sqrt(TOKENS)
    width, columns = w_up.shape
    x = lax.axis_index("x")
    place = lax.axis_index(DP)
    exact = lax.Precision.HIGHEST
    with jax.named_scope("token_gather"):
        pair = pair_y(cotangent)
        mine = spread(tokens, ("yl", "z"), 32)
        cot = gather_x(pair)
        mine = after(mine, *cot)
        other = swap(mine, "c", 1)
    with jax.named_scope("local_work"):
        at = jnp.stack([place, lax.axis_index("c"), x]).astype(jnp.int32)
        joined, total, near, opposite, far, sent = local_work(at, mine, other, norm_gain[None], w_up)
    with jax.named_scope("sums_x"):
        got = spread(sent, MP, 8)
        moved = [swap(v, "x", b) for b, v in ((1, near), (2, opposite), (3, far))]
        got = after(got, *moved).astype(F32)
        total = total + sum(m.astype(F32) for m in moved)
    with jax.named_scope("stats"):
        local = got[:, 16] + got[:, 17] + got[:, 18]
        css = got[:, 19] + got[:, 20]
        lean = got[:, 21] + got[:, 22]
        column = got[:, 23, :columns] + got[:, 23, columns : 2 * columns]
        power = got[:, 23, 2 * columns : 2 * columns + 1] + got[:, 23, 2 * columns + 128 : 2 * columns + 129]
        mean = jnp.sum(local, axis=0) / 8
        apart = local - mean[None, :]
        var = (jnp.sum(css, axis=0) + width * jnp.sum(apart * apart, axis=0)) / D
        inv = lax.rsqrt(var + 1e-06)
    with jax.named_scope("gram"):
        left = jnp.concatenate([lean, apart, power * apart], axis=0) * inv[None, :]
        left = lax.dynamic_slice_in_dim(left, place * 16, 16, 1)
        own = lax.dynamic_slice_in_dim(inv, place * 16, 16, 0)
        right = jnp.concatenate([apart, lean, apart], axis=0)
        rows = jnp.sum(got[:, :16], axis=0) * own[:, None] + dot(left, right, ((0,), (0,)), exact)
        rows = (rows * inv[None, :]).astype(BF)
        half = total.astype(BF)
        moved = swap(half, "yh", 1)
        gram = jnp.stack(ordered([rows] + [swap(rows, "yl", b) for b in (1, 2, 3)], lax.axis_index("yl")))
        gram = spread(gram, ("z",), 8)
    with jax.named_scope("pre"):
        normed = joined.reshape(TOKENS, width).astype(F32) - mean[:, None]
        normed = (normed * inv[:, None] * norm_gain[None, :]).astype(BF)
        shift = dot(lax.dynamic_slice_in_dim(apart, x * 256, 256, 1), column, ((0,), (0,)), exact)
        total = total + shift
        total = (total + after(moved, normed).astype(F32)) * lax.dynamic_slice_in_dim(inv, x * 256, 256, 0)[:, None]
        moved = gather_x(total.astype(BF))
        cot = jnp.stack(ordered(cot, x), axis=1).reshape(TOKENS, columns)
        gram = join_cores(after(gram, *moved).reshape(32, 16, TOKENS)).reshape(8, 4, 32, TOKENS)
        gram = jnp.swapaxes(gram, 0, 1).reshape(TOKENS, TOKENS)
        pre = jnp.concatenate(ordered(moved, x), axis=0).astype(F32)

    def slope_at(value):
        return (cot.astype(F32) * gelu_slope(value) * scale).astype(BF)

    with jax.named_scope("ascent"):
        slope = slope_at(pre)
        along = dot(gram, slope, ((1,), (0,)))
        squared = jnp.sum(slope.astype(F32) * along)
        squared = jnp.sum(spread(jnp.full((1, 128), squared), DP, 64)[:, 0, 0])
        size = jnp.sqrt(jnp.maximum(squared, 0.0)) + 1e-12
        radius = 0.5 * math.sqrt(FF)
    with jax.named_scope("sharp"):
        sharp = slope_at(pre + along * (radius / size))
        return dot(normed, sharp, ((0,), (0,)))


def solution(mesh):
    fine = Mesh(mesh.devices.reshape(4, 8, 2, 2, 4), DP + MP)
    placed = (P(DP, MP), P(MP), P(MP, DP), P(MP, DP))
    return jax.shard_map(
        per_device, mesh=fine, in_specs=placed, out_specs=P(MP, DP), check_vma=False
    )
```

```python
import math

import jax
import jax.numpy as jnp
from jax import lax
from jax.experimental import pallas as pl
from jax.experimental.pallas import tpu as pltpu
from jax.sharding import Mesh
from jax.sharding import PartitionSpec as P

FF = 24576
D = 6144
TOKENS = 1024
DP = ("yl", "z", "c")
MP = ("yh", "x")
BF = jnp.bfloat16
F32 = jnp.float32


def gelu_slope(value):
    cdf = 0.5 * (1.0 + lax.erf(value * (1.0 / math.sqrt(2.0))))
    dens = jnp.exp(-0.5 * value * value) * (1.0 / math.sqrt(2.0 * math.pi))
    return cdf + value * dens


def swap(value, axis, bit):
    size = lax.axis_size(axis)
    return lax.ppermute(value, axis, [(i, i ^ bit) for i in range(size)])


def spread(value, axes, count):
    copies = jnp.broadcast_to(value[None], (count,) + value.shape)
    return lax.all_to_all(copies, axes, 0, 0, tiled=True)


def after(value, *others):
    return lax.optimization_barrier((value,) + others)[0]


def gather_x(value):
    return [value] + [swap(value, "x", b) for b in (1, 2, 3)]


def dot(left, right, dims, precision=None):
    return lax.dot_general(left, right, (dims, ((), ())), precision=precision, preferred_element_type=F32)


def split(value, count):
    out = []
    for _ in range(count):
        out.append(value.astype(BF).astype(F32))
        value = value - out[-1]
    return out


def local_kernel(at, mine, other, gain, w, joined, own, near, opposite, far, sent, high, part, out, sems):
    place, core, x = at[0], at[1], at[2]
    g = gain[...]
    width = g.shape[1]
    ones = jnp.ones((8, width), BF)
    gains = jnp.concatenate(split(g, 3) + [jnp.zeros((5, width), F32)], axis=0).astype(BF)
    local, css, lean = [], [], []
    for i in range(8):
        chips = pl.ds(4 * i, 4)
        joined[chips, core] = mine[chips]
        joined[chips, 1 - core] = other[chips]
        raw = joined[chips].reshape(128, width)
        value = raw.astype(F32)
        centred = value - jnp.sum(value, axis=1, keepdims=True) * (1.0 / width)
        full = centred * g
        first = full.astype(BF)
        second = (full - first.astype(F32)).astype(BF)
        high[pl.ds(128 * i, 128)] = first
        rows = dot(first, w[...], ((1,), (0,))) + dot(second, w[...], ((1,), (0,)))
        part[i // 2, pl.ds(128 * (i % 2), 128)] = rows
        square = centred * centred
        top = square.astype(BF)
        rest = (square - top.astype(F32)).astype(BF)
        across = ((1,), (1,))
        local.append(dot(ones, raw, across)[:1] * (1.0 / width))
        css.append((dot(ones, top, across) + dot(ones, rest, across))[:1])
        lean.append(jnp.sum(dot(gains, first, across), axis=0, keepdims=True))
    own[...] = part[x]
    copies = []
    for b, target in ((1, near), (2, opposite), (3, far)):
        out[b - 1] = part[x ^ b].astype(BF)
        copies.append(pltpu.make_async_copy(out.at[b - 1], target, sems.at[b - 1]))
        copies[-1].start()
    gram = dot(high[pl.ds(pl.multiple_of(place * 16, 16), 16)], high[...], ((1,), (1,)))
    local, css, lean = (jnp.concatenate(v, axis=1) for v in (local, css, lean))
    column = jnp.sum(dot(gains, w[...], ((1,), (0,))), axis=0, keepdims=True)
    power = jnp.broadcast_to(jnp.sum(g * g, axis=1, keepdims=True), (1, 128))
    extra = jnp.concatenate(split(column, 2) + split(power, 2), axis=1)
    rows = [gram] + split(local, 3) + split(css, 2) + split(lean, 2) + [extra]
    sent[...] = jnp.concatenate(rows, axis=0).astype(BF)
    for copy in copies:
        copy.wait()


def local_work(at, mine, other, gain, w):
    width, columns = w.shape
    block = jax.ShapeDtypeStruct((256, columns), BF)
    vmem = pl.BlockSpec(memory_space=pltpu.VMEM)
    return pl.pallas_call(
        local_kernel,
        out_shape=[
            jax.ShapeDtypeStruct((32, 2, 16, width), BF),
            jax.ShapeDtypeStruct((256, columns), F32),
            block,
            block,
            block,
            jax.ShapeDtypeStruct((24, TOKENS), BF),
        ],
        in_specs=[pl.BlockSpec(memory_space=pltpu.SMEM)] + [vmem] * 4,
        out_specs=[vmem] * 2 + [pl.BlockSpec(memory_space=pl.ANY)] * 3 + [vmem],
        scratch_shapes=[
            pltpu.VMEM((TOKENS, width), BF),
            pltpu.VMEM((4, 256, columns), F32),
            pltpu.VMEM((3, 256, columns), BF),
            pltpu.SemaphoreType.DMA((3,)),
        ],
        compiler_params=pltpu.CompilerParams(vmem_limit_bytes=40 << 20),
        cost_estimate=pl.CostEstimate(flops=2 * TOKENS * width * columns * 2, bytes_accessed=8 << 20, transcendentals=0),
        name="local_work",
    )(at, mine, other, gain, w)


def stats_kernel(at, got, own, one, two, three, cot, cot_other, rows, half, full, pair, scales, turned):
    place, x, low = at[0], at[2], at[3] == 0
    exact = lax.Precision.HIGHEST
    columns = own.shape[1]
    total = own[...] + one[...].astype(F32) + two[...].astype(F32) + three[...].astype(F32)
    half[...] = total.astype(BF)
    pair[at[3]] = cot[...]
    pair[1 - at[3]] = cot_other[...]
    gram = got[0, :16].astype(F32)
    for j in range(1, 8):
        gram = gram + got[j, :16].astype(F32)
    terms = [got[j, 16:24].astype(F32) for j in range(8)]
    local = jnp.concatenate([t[0:1] + t[1:2] + t[2:3] for t in terms], axis=0)
    css = jnp.concatenate([t[3:4] + t[4:5] for t in terms], axis=0)
    lean = jnp.concatenate([t[5:6] + t[6:7] for t in terms], axis=0)
    column = jnp.concatenate([t[7:8, :columns] + t[7:8, columns : 2 * columns] for t in terms], axis=0)
    power = jnp.concatenate([t[7:8, 2 * columns : 2 * columns + 1] + t[7:8, 2 * columns + 128 : 2 * columns + 129] for t in terms], axis=0)
    mean = jnp.sum(local, axis=0, keepdims=True) / 8
    apart = local - mean
    var = (jnp.sum(css, axis=0, keepdims=True) + (D // 8) * jnp.sum(apart * apart, axis=0, keepdims=True)) / D
    inv = lax.rsqrt(var + 1e-06)
    flat = jnp.concatenate([lean, apart, power * apart, apart, inv, mean, jnp.zeros((94, TOKENS), F32)], axis=0)
    turned[...] = flat.T
    mine = turned[pl.ds(pl.multiple_of(place * 16, 16), 16)]
    right = jnp.concatenate([apart, lean, apart], axis=0)
    gram = (gram + dot(mine[:, :24], right, ((1,), (0,)), exact)) * mine[:, 32:33] * inv
    rows[...] = gram.astype(BF)
    here = turned[pl.ds(pl.multiple_of(x * 256, 256), 256)]
    full[...] = total + dot(here[:, 24:32], column, ((1,), (0,)), exact)
    scales[...] = turned[...]


def stats_work(at, got, own, moved, cot, cot_other):
    columns = own.shape[1]
    vmem = pl.BlockSpec(memory_space=pltpu.VMEM)
    return pl.pallas_call(
        stats_kernel,
        out_shape=[
            jax.ShapeDtypeStruct((16, TOKENS), BF),
            jax.ShapeDtypeStruct((256, columns), BF),
            jax.ShapeDtypeStruct((256, columns), F32),
            jax.ShapeDtypeStruct((2, 128, columns), BF),
            jax.ShapeDtypeStruct((TOKENS, 128), F32),
        ],
        in_specs=[pl.BlockSpec(memory_space=pltpu.SMEM)] + [vmem] * 7,
        out_specs=[vmem] * 5,
        scratch_shapes=[pltpu.VMEM((TOKENS, 128), F32)],
        compiler_params=pltpu.CompilerParams(vmem_limit_bytes=40 << 20),
        cost_estimate=pl.CostEstimate(flops=10 << 20, bytes_accessed=3 << 20, transcendentals=0),
        name="stats_work",
    )(at, got, own, *moved, cot, cot_other)


def pre_kernel(at, full, moved, scales, one, two, three, out):
    inv = scales[pl.ds(pl.multiple_of(at[2] * 256, 256), 256)][:, 32:33]
    out[...] = ((full[...] + moved[...].astype(F32)) * inv).astype(BF)


def pre_work(at, full, moved, scales, cots):
    vmem = pl.BlockSpec(memory_space=pltpu.VMEM)
    return pl.pallas_call(
        pre_kernel,
        out_shape=jax.ShapeDtypeStruct(full.shape, BF),
        in_specs=[pl.BlockSpec(memory_space=pltpu.SMEM)] + [vmem] * 3 + [pl.BlockSpec(memory_space=pl.ANY)] * 3,
        out_specs=vmem,
        compiler_params=pltpu.CompilerParams(vmem_limit_bytes=40 << 20),
        cost_estimate=pl.CostEstimate(flops=1 << 20, bytes_accessed=1 << 20, transcendentals=0),
        name="pre_work",
    )(at, full, moved, scales, *cots)


def slope_of(cot, value):
    return (cot.astype(F32) * gelu_slope(value) * (1.0 / math.sqrt(TOKENS))).astype(BF)


def ascent_kernel(at, mine, other, p0, p1, p2, p3, c0, c1, c2, c3, along, pre, cot, squared, slope):
    core, x = at[1], at[2]
    columns = p0.shape[1]
    for b, (p, c) in enumerate(((p0, c0), (p1, c1), (p2, c2), (p3, c3))):
        q = x ^ b
        pre[pl.ds(pl.multiple_of(q * 256, 256), 256)] = p[...]
        cot[pl.ds(pl.multiple_of(q * 128, 128), 128)] = c[0]
        cot[pl.ds(pl.multiple_of(512 + q * 128, 128), 128)] = c[1]
    for i in range(8):
        rows = pl.ds(128 * i, 128)
        value = slope_of(cot[rows], pre[rows].astype(F32))
        slope[pl.ds(4 * i, 4)] = value.reshape(4, 2, 16, columns)
    total = jnp.zeros((1, 1), F32)
    for gram, c in ((mine, core), (other, 1 - core)):
        for i in range(2):
            chips = pl.ds(16 * i, 16)
            part = dot(gram[chips].reshape(256, TOKENS), slope[...].reshape(TOKENS, columns), ((1,), (0,)))
            along[chips, c] = part.reshape(16, 16, columns)
            weighed = part * slope[chips, c].reshape(256, columns).astype(F32)
            total = total + jnp.sum(jnp.sum(weighed, axis=0, keepdims=True), axis=1, keepdims=True)
    squared[...] = jnp.broadcast_to(total.reshape(1, 1, 1), squared.shape)


def ascent_work(at, mine, other, pres, cots):
    columns = pres[0].shape[1]
    vmem = pl.BlockSpec(memory_space=pltpu.VMEM)
    flat = jax.ShapeDtypeStruct((TOKENS, columns), BF)
    return pl.pallas_call(
        ascent_kernel,
        out_shape=[
            jax.ShapeDtypeStruct((32, 2, 16, columns), F32),
            flat,
            flat,
            jax.ShapeDtypeStruct((64, 1, 128), F32),
        ],
        in_specs=[pl.BlockSpec(memory_space=pltpu.SMEM)] + [vmem] * 10,
        out_specs=[vmem] * 4,
        scratch_shapes=[pltpu.VMEM((32, 2, 16, columns), BF)],
        compiler_params=pltpu.CompilerParams(vmem_limit_bytes=40 << 20),
        cost_estimate=pl.CostEstimate(flops=2 * TOKENS * TOKENS * columns, bytes_accessed=8 << 20, transcendentals=2 * TOKENS * columns),
        name="ascent_work",
    )(at, mine, other, *pres, *cots)


def per_device(tokens, norm_gain, w_up, cotangent):
    width, columns = w_up.shape
    places = (lax.axis_index(DP), lax.axis_index("c"), lax.axis_index("x"), lax.axis_index("yh"))
    at = jnp.stack(places).astype(jnp.int32)
    with jax.named_scope("token_gather"):
        mine = spread(tokens, ("yl", "z"), 32)
        other = swap(mine, "c", 1)
        cot_other = swap(after(cotangent, mine[0, 0, :128]), "yh", 1)
    with jax.named_scope("local_work"):
        joined, own, near, opposite, far, sent = local_work(at, mine, other, norm_gain[None], w_up)
    with jax.named_scope("sums_x"):
        got = spread(sent, MP, 8)
        moved = [swap(v, "x", b) for b, v in ((1, near), (2, opposite), (3, far))]
    with jax.named_scope("stats_work"):
        rows, half, full, pair, scales = stats_work(at, got, own, moved, cotangent, cot_other)
        normed = joined.reshape(TOKENS, width).astype(F32) - scales[:, 33:34]
        normed = (normed * scales[:, 32:33] * norm_gain[None, :]).astype(BF)
    with jax.named_scope("gram_gather"):
        gram = spread(rows, ("yl", "z"), 32)
        gram_other = swap(gram, "c", 1)
    with jax.named_scope("pre"):
        moved = swap(half, "yh", 1)
        cots = gather_x(pair)
        pres = gather_x(pre_work(at, full, moved, scales, cots[1:]))
    with jax.named_scope("ascent"):
        along, pre, cot, squared = ascent_work(at, gram, gram_other, pres, cots)
        squared = jnp.sum(lax.all_to_all(squared, DP, 0, 0, tiled=True)[:, 0, 0])
        size = jnp.sqrt(jnp.maximum(squared, 0.0)) + 1e-12
        radius = 0.5 * math.sqrt(FF)
    with jax.named_scope("sharp"):
        sharp = slope_of(cot, pre.astype(F32) + along.reshape(TOKENS, columns) * (radius / size))
        return dot(normed, sharp, ((0,), (0,)))


def solution(mesh):
    fine = Mesh(mesh.devices.reshape(4, 8, 2, 2, 4), DP + MP)
    placed = (P(DP, MP), P(MP), P(MP, DP), P(MP, DP))
    return jax.shard_map(
        per_device, mesh=fine, in_specs=placed, out_specs=P(MP, DP), check_vma=False
    )
```

```python
import math

import jax
import jax.numpy as jnp
from jax import lax
from jax.experimental import pallas as pl
from jax.experimental.pallas import tpu as pltpu
from jax.sharding import Mesh
from jax.sharding import PartitionSpec as P

FF = 24576
D = 6144
TOKENS = 1024
DP = ("yl", "z", "c")
MP = ("yh", "x")
BF = jnp.bfloat16
F32 = jnp.float32


def gelu_slope(value):
    cdf = 0.5 * (1.0 + lax.erf(value * (1.0 / math.sqrt(2.0))))
    dens = jnp.exp(-0.5 * value * value) * (1.0 / math.sqrt(2.0 * math.pi))
    return cdf + value * dens


def swap(value, axis, bit):
    size = lax.axis_size(axis)
    return lax.ppermute(value, axis, [(i, i ^ bit) for i in range(size)])


def spread(value, axes, count):
    copies = jnp.broadcast_to(value[None], (count,) + value.shape)
    return lax.all_to_all(copies, axes, 0, 0, tiled=True)


def after(value, *others):
    return lax.optimization_barrier((value,) + others)[0]


def gather_x(value):
    return [value] + [swap(value, "x", b) for b in (1, 2, 3)]


def dot(left, right, dims, precision=None):
    return lax.dot_general(left, right, (dims, ((), ())), precision=precision, preferred_element_type=F32)


def split(value, count):
    out = []
    for _ in range(count):
        out.append(value.astype(BF).astype(F32))
        value = value - out[-1]
    return out


def local_kernel(at, mine, other, gain, w, joined, own, near, opposite, far, sent, high, part, out, sems):
    place, core, x = at[0], at[1], at[2]
    g = gain[...]
    width = g.shape[1]
    ones = jnp.ones((8, width), BF)
    gains = jnp.concatenate(split(g, 3) + [jnp.zeros((5, width), F32)], axis=0).astype(BF)
    local, css, lean = [], [], []
    for i in range(8):
        chips = pl.ds(4 * i, 4)
        joined[chips, core] = mine[chips]
        joined[chips, 1 - core] = other[chips]
        raw = joined[chips].reshape(128, width)
        value = raw.astype(F32)
        centred = value - jnp.sum(value, axis=1, keepdims=True) * (1.0 / width)
        full = centred * g
        first = full.astype(BF)
        second = (full - first.astype(F32)).astype(BF)
        high[pl.ds(128 * i, 128)] = first
        rows = dot(first, w[...], ((1,), (0,))) + dot(second, w[...], ((1,), (0,)))
        part[i // 2, pl.ds(128 * (i % 2), 128)] = rows
        square = centred * centred
        top = square.astype(BF)
        rest = (square - top.astype(F32)).astype(BF)
        across = ((1,), (1,))
        local.append(dot(ones, raw, across)[:1] * (1.0 / width))
        css.append((dot(ones, top, across) + dot(ones, rest, across))[:1])
        lean.append(jnp.sum(dot(gains, first, across), axis=0, keepdims=True))
    own[...] = part[x]
    copies = []
    for b, target in ((1, near), (2, opposite), (3, far)):
        out[b - 1] = part[x ^ b].astype(BF)
        copies.append(pltpu.make_async_copy(out.at[b - 1], target, sems.at[b - 1]))
        copies[-1].start()
    gram = dot(high[pl.ds(pl.multiple_of(place * 16, 16), 16)], high[...], ((1,), (1,)))
    local, css, lean = (jnp.concatenate(v, axis=1) for v in (local, css, lean))
    column = jnp.sum(dot(gains, w[...], ((1,), (0,))), axis=0, keepdims=True)
    power = jnp.broadcast_to(jnp.sum(g * g, axis=1, keepdims=True), (1, 128))
    extra = jnp.concatenate(split(column, 2) + split(power, 2), axis=1)
    rows = [gram] + split(local, 3) + split(css, 2) + split(lean, 2) + [extra]
    sent[...] = jnp.concatenate(rows, axis=0).astype(BF)
    for copy in copies:
        copy.wait()


def local_work(at, mine, other, gain, w):
    width, columns = w.shape
    block = jax.ShapeDtypeStruct((256, columns), BF)
    vmem = pl.BlockSpec(memory_space=pltpu.VMEM)
    return pl.pallas_call(
        local_kernel,
        out_shape=[
            jax.ShapeDtypeStruct((32, 2, 16, width), BF),
            jax.ShapeDtypeStruct((256, columns), F32),
            block,
            block,
            block,
            jax.ShapeDtypeStruct((24, TOKENS), BF),
        ],
        in_specs=[pl.BlockSpec(memory_space=pltpu.SMEM)] + [vmem] * 4,
        out_specs=[vmem] * 2 + [pl.BlockSpec(memory_space=pl.ANY)] * 3 + [vmem],
        scratch_shapes=[
            pltpu.VMEM((TOKENS, width), BF),
            pltpu.VMEM((4, 256, columns), F32),
            pltpu.VMEM((3, 256, columns), BF),
            pltpu.SemaphoreType.DMA((3,)),
        ],
        compiler_params=pltpu.CompilerParams(vmem_limit_bytes=40 << 20),
        cost_estimate=pl.CostEstimate(flops=2 * TOKENS * width * columns * 2, bytes_accessed=8 << 20, transcendentals=0),
        name="local_work",
    )(at, mine, other, gain, w)


def stats_kernel(at, got, own, one, two, three, cot, cot_other, rows, half, full, pair, scales, turned):
    place, x, low = at[0], at[2], at[3] == 0
    exact = lax.Precision.HIGHEST
    columns = own.shape[1]
    total = own[...] + one[...].astype(F32) + two[...].astype(F32) + three[...].astype(F32)
    half[...] = total.astype(BF)
    pair[at[3]] = cot[...]
    pair[1 - at[3]] = cot_other[...]
    gram = got[0, :16].astype(F32)
    for j in range(1, 8):
        gram = gram + got[j, :16].astype(F32)
    terms = [got[j, 16:24].astype(F32) for j in range(8)]
    local = jnp.concatenate([t[0:1] + t[1:2] + t[2:3] for t in terms], axis=0)
    css = jnp.concatenate([t[3:4] + t[4:5] for t in terms], axis=0)
    lean = jnp.concatenate([t[5:6] + t[6:7] for t in terms], axis=0)
    column = jnp.concatenate([t[7:8, :columns] + t[7:8, columns : 2 * columns] for t in terms], axis=0)
    power = jnp.concatenate([t[7:8, 2 * columns : 2 * columns + 1] + t[7:8, 2 * columns + 128 : 2 * columns + 129] for t in terms], axis=0)
    mean = jnp.sum(local, axis=0, keepdims=True) / 8
    apart = local - mean
    var = (jnp.sum(css, axis=0, keepdims=True) + (D // 8) * jnp.sum(apart * apart, axis=0, keepdims=True)) / D
    inv = lax.rsqrt(var + 1e-06)
    flat = jnp.concatenate([lean, apart, power * apart, apart, inv, mean, jnp.zeros((94, TOKENS), F32)], axis=0)
    turned[...] = flat.T
    mine = turned[pl.ds(pl.multiple_of(place * 16, 16), 16)]
    right = jnp.concatenate([apart, lean, apart], axis=0)
    gram = (gram + dot(mine[:, :24], right, ((1,), (0,)), exact)) * mine[:, 32:33] * inv
    rows[...] = gram.astype(BF)
    here = turned[pl.ds(pl.multiple_of(x * 256, 256), 256)]
    full[...] = total + dot(here[:, 24:32], column, ((1,), (0,)), exact)
    scales[...] = turned[...]


def stats_work(at, got, own, moved, cot, cot_other):
    columns = own.shape[1]
    vmem = pl.BlockSpec(memory_space=pltpu.VMEM)
    return pl.pallas_call(
        stats_kernel,
        out_shape=[
            jax.ShapeDtypeStruct((16, TOKENS), BF),
            jax.ShapeDtypeStruct((256, columns), BF),
            jax.ShapeDtypeStruct((256, columns), F32),
            jax.ShapeDtypeStruct((2, 128, columns), BF),
            jax.ShapeDtypeStruct((TOKENS, 128), F32),
        ],
        in_specs=[pl.BlockSpec(memory_space=pltpu.SMEM)] + [vmem] * 7,
        out_specs=[vmem] * 5,
        scratch_shapes=[pltpu.VMEM((TOKENS, 128), F32)],
        compiler_params=pltpu.CompilerParams(vmem_limit_bytes=40 << 20),
        cost_estimate=pl.CostEstimate(flops=10 << 20, bytes_accessed=3 << 20, transcendentals=0),
        name="stats_work",
    )(at, got, own, *moved, cot, cot_other)


def pre_kernel(at, full, moved, scales, one, two, three, out):
    inv = scales[pl.ds(pl.multiple_of(at[2] * 256, 256), 256)][:, 32:33]
    out[...] = ((full[...] + moved[...].astype(F32)) * inv).astype(BF)


def pre_work(at, full, moved, scales, cots):
    vmem = pl.BlockSpec(memory_space=pltpu.VMEM)
    return pl.pallas_call(
        pre_kernel,
        out_shape=jax.ShapeDtypeStruct(full.shape, BF),
        in_specs=[pl.BlockSpec(memory_space=pltpu.SMEM)] + [vmem] * 3 + [pl.BlockSpec(memory_space=pl.ANY)] * 3,
        out_specs=vmem,
        compiler_params=pltpu.CompilerParams(vmem_limit_bytes=40 << 20),
        cost_estimate=pl.CostEstimate(flops=1 << 20, bytes_accessed=1 << 20, transcendentals=0),
        name="pre_work",
    )(at, full, moved, scales, *cots)


def slope_of(cot, value):
    return (cot.astype(F32) * gelu_slope(value) * (1.0 / math.sqrt(TOKENS))).astype(BF)


def ascent_kernel(at, mine, other, p0, p1, p2, p3, c0, c1, c2, c3, along, pre, cot, squared, slope):
    core, x = at[1], at[2]
    columns = p0.shape[1]
    for b, (p, c) in enumerate(((p0, c0), (p1, c1), (p2, c2), (p3, c3))):
        q = x ^ b
        pre[pl.ds(pl.multiple_of(q * 256, 256), 256)] = p[...]
        cot[pl.ds(pl.multiple_of(q * 128, 128), 128)] = c[0]
        cot[pl.ds(pl.multiple_of(512 + q * 128, 128), 128)] = c[1]
    for i in range(8):
        rows = pl.ds(128 * i, 128)
        value = slope_of(cot[rows], pre[rows].astype(F32))
        slope[pl.ds(4 * i, 4)] = value.reshape(4, 2, 16, columns)
    total = jnp.zeros((1, 1), F32)
    for gram, c in ((mine, core), (other, 1 - core)):
        for i in range(2):
            chips = pl.ds(16 * i, 16)
            part = dot(gram[chips].reshape(256, TOKENS), slope[...].reshape(TOKENS, columns), ((1,), (0,)))
            along[chips, c] = part.reshape(16, 16, columns)
            weighed = part * slope[chips, c].reshape(256, columns).astype(F32)
            total = total + jnp.sum(jnp.sum(weighed, axis=0, keepdims=True), axis=1, keepdims=True)
    squared[...] = jnp.broadcast_to(total.reshape(1, 1, 1), squared.shape)


def ascent_work(at, mine, other, pres, cots):
    columns = pres[0].shape[1]
    vmem = pl.BlockSpec(memory_space=pltpu.VMEM)
    flat = jax.ShapeDtypeStruct((TOKENS, columns), BF)
    return pl.pallas_call(
        ascent_kernel,
        out_shape=[
            jax.ShapeDtypeStruct((32, 2, 16, columns), F32),
            flat,
            flat,
            jax.ShapeDtypeStruct((64, 1, 128), F32),
        ],
        in_specs=[pl.BlockSpec(memory_space=pltpu.SMEM)] + [vmem] * 10,
        out_specs=[vmem] * 4,
        scratch_shapes=[pltpu.VMEM((32, 2, 16, columns), BF)],
        compiler_params=pltpu.CompilerParams(vmem_limit_bytes=40 << 20),
        cost_estimate=pl.CostEstimate(flops=2 * TOKENS * TOKENS * columns, bytes_accessed=8 << 20, transcendentals=2 * TOKENS * columns),
        name="ascent_work",
    )(at, mine, other, *pres, *cots)


def per_device(tokens, norm_gain, w_up, cotangent):
    width, columns = w_up.shape
    places = (lax.axis_index(DP), lax.axis_index("c"), lax.axis_index("x"), lax.axis_index("yh"))
    at = jnp.stack(places).astype(jnp.int32)
    with jax.named_scope("token_gather"):
        mine = spread(tokens, ("yl", "z"), 32)
        other = swap(mine, "c", 1)
        cot_other = swap(after(cotangent, mine[0, 0, :128]), "yh", 1)
    with jax.named_scope("local_work"):
        joined, own, near, opposite, far, sent = local_work(at, mine, other, norm_gain[None], w_up)
    with jax.named_scope("sums_x"):
        got = spread(after(sent, cot_other[0, :128]), MP, 8)
        moved = [swap(v, "x", b) for b, v in ((1, near), (2, opposite), (3, far))]
    with jax.named_scope("stats_work"):
        rows, half, full, pair, scales = stats_work(at, got, own, moved, cotangent, cot_other)
        normed = joined.reshape(TOKENS, width).astype(F32) - scales[:, 33:34]
        normed = (normed * scales[:, 32:33] * norm_gain[None, :]).astype(BF)
    with jax.named_scope("gram_gather"):
        gram = spread(rows, ("yl", "z"), 32)
    with jax.named_scope("pre"):
        moved = swap(half, "yh", 1)
        cots = gather_x(pair)
        pres = gather_x(pre_work(at, full, moved, scales, cots[1:]))
        gram = after(gram, pres[1][0, :128])
        gram_other = swap(gram, "c", 1)
    with jax.named_scope("ascent"):
        along, pre, cot, squared = ascent_work(at, gram, gram_other, pres, cots)
        squared = jnp.sum(lax.all_to_all(squared, DP, 0, 0, tiled=True)[:, 0, 0])
        size = jnp.sqrt(jnp.maximum(squared, 0.0)) + 1e-12
        radius = 0.5 * math.sqrt(FF)
    with jax.named_scope("sharp"):
        sharp = slope_of(cot, pre.astype(F32) + along.reshape(TOKENS, columns) * (radius / size))
        return dot(normed, sharp, ((0,), (0,)))


def solution(mesh):
    fine = Mesh(mesh.devices.reshape(4, 8, 2, 2, 4), DP + MP)
    placed = (P(DP, MP), P(MP), P(MP, DP), P(MP, DP))
    return jax.shard_map(
        per_device, mesh=fine, in_specs=placed, out_specs=P(MP, DP), check_vma=False
    )
```

```python
import math

import jax
import jax.numpy as jnp
from jax import lax
from jax.experimental import pallas as pl
from jax.experimental.pallas import tpu as pltpu
from jax.sharding import Mesh
from jax.sharding import PartitionSpec as P

FF = 24576
D = 6144
TOKENS = 1024
DP = ("yl", "z", "c")
MP = ("yh", "x")
BF = jnp.bfloat16
F32 = jnp.float32


def gelu_slope(value):
    cdf = 0.5 * (1.0 + lax.erf(value * (1.0 / math.sqrt(2.0))))
    dens = jnp.exp(-0.5 * value * value) * (1.0 / math.sqrt(2.0 * math.pi))
    return cdf + value * dens


def swap(value, axis, bit):
    size = lax.axis_size(axis)
    return lax.ppermute(value, axis, [(i, i ^ bit) for i in range(size)])


def spread(value, axes, count):
    copies = jnp.broadcast_to(value[None], (count,) + value.shape)
    return lax.all_to_all(copies, axes, 0, 0, tiled=True)


def gather_x(value):
    return [value] + [swap(value, "x", b) for b in (1, 2, 3)]


def dot(left, right, dims, precision=None):
    return lax.dot_general(left, right, (dims, ((), ())), precision=precision, preferred_element_type=F32)


def split(value, count):
    out = []
    for _ in range(count):
        out.append(value.astype(BF).astype(F32))
        value = value - out[-1]
    return out


def local_kernel(at, mine, other, gain, w, joined, own, near, opposite, far, sent, high, part, out, sems):
    place, core, x = at[0], at[1], at[2]
    g = gain[...]
    width = g.shape[1]
    ones = jnp.ones((8, width), BF)
    gains = jnp.concatenate(split(g, 3) + [jnp.zeros((5, width), F32)], axis=0).astype(BF)
    local, css, lean = [], [], []
    for i in range(8):
        chips = pl.ds(4 * i, 4)
        joined[chips, core] = mine[chips]
        joined[chips, 1 - core] = other[chips]
        raw = joined[chips].reshape(128, width)
        value = raw.astype(F32)
        centred = value - jnp.sum(value, axis=1, keepdims=True) * (1.0 / width)
        full = centred * g
        first = full.astype(BF)
        second = (full - first.astype(F32)).astype(BF)
        high[pl.ds(128 * i, 128)] = first
        rows = dot(first, w[...], ((1,), (0,))) + dot(second, w[...], ((1,), (0,)))
        part[i // 2, pl.ds(128 * (i % 2), 128)] = rows
        square = centred * centred
        top = square.astype(BF)
        rest = (square - top.astype(F32)).astype(BF)
        across = ((1,), (1,))
        local.append(dot(ones, raw, across)[:1] * (1.0 / width))
        css.append((dot(ones, top, across) + dot(ones, rest, across))[:1])
        lean.append(jnp.sum(dot(gains, first, across), axis=0, keepdims=True))
    own[...] = part[x]
    copies = []
    for b, target in ((1, near), (2, opposite), (3, far)):
        out[b - 1] = part[x ^ b].astype(BF)
        copies.append(pltpu.make_async_copy(out.at[b - 1], target, sems.at[b - 1]))
        copies[-1].start()
    gram = dot(high[pl.ds(pl.multiple_of(place * 16, 16), 16)], high[...], ((1,), (1,)))
    local, css, lean = (jnp.concatenate(v, axis=1) for v in (local, css, lean))
    column = jnp.sum(dot(gains, w[...], ((1,), (0,))), axis=0, keepdims=True)
    power = jnp.broadcast_to(jnp.sum(g * g, axis=1, keepdims=True), (1, 128))
    extra = jnp.concatenate(split(column, 2) + split(power, 2), axis=1)
    rows = [gram] + split(local, 3) + split(css, 2) + split(lean, 2) + [extra]
    sent[...] = jnp.concatenate(rows, axis=0).astype(BF)
    for copy in copies:
        copy.wait()


def local_work(at, mine, other, gain, w):
    width, columns = w.shape
    block = jax.ShapeDtypeStruct((256, columns), BF)
    vmem = pl.BlockSpec(memory_space=pltpu.VMEM)
    return pl.pallas_call(
        local_kernel,
        out_shape=[
            jax.ShapeDtypeStruct((32, 2, 16, width), BF),
            jax.ShapeDtypeStruct((256, columns), F32),
            block,
            block,
            block,
            jax.ShapeDtypeStruct((24, TOKENS), BF),
        ],
        in_specs=[pl.BlockSpec(memory_space=pltpu.SMEM)] + [vmem] * 4,
        out_specs=[vmem] * 2 + [pl.BlockSpec(memory_space=pl.ANY)] * 3 + [vmem],
        scratch_shapes=[
            pltpu.VMEM((TOKENS, width), BF),
            pltpu.VMEM((4, 256, columns), F32),
            pltpu.VMEM((3, 256, columns), BF),
            pltpu.SemaphoreType.DMA((3,)),
        ],
        compiler_params=pltpu.CompilerParams(vmem_limit_bytes=40 << 20),
        cost_estimate=pl.CostEstimate(flops=2 * TOKENS * width * columns * 2, bytes_accessed=8 << 20, transcendentals=0),
        name="local_work",
    )(at, mine, other, gain, w)


def stats_kernel(at, got, own, one, two, three, cot, cot_other, rows, half, full, pair, scales, turned):
    place, x, low = at[0], at[2], at[3] == 0
    exact = lax.Precision.HIGHEST
    columns = own.shape[1]
    total = own[...] + one[...].astype(F32) + two[...].astype(F32) + three[...].astype(F32)
    half[...] = total.astype(BF)
    pair[at[3]] = cot[...]
    pair[1 - at[3]] = cot_other[...]
    gram = got[0, :16].astype(F32)
    for j in range(1, 8):
        gram = gram + got[j, :16].astype(F32)
    terms = [got[j, 16:24].astype(F32) for j in range(8)]
    local = jnp.concatenate([t[0:1] + t[1:2] + t[2:3] for t in terms], axis=0)
    css = jnp.concatenate([t[3:4] + t[4:5] for t in terms], axis=0)
    lean = jnp.concatenate([t[5:6] + t[6:7] for t in terms], axis=0)
    column = jnp.concatenate([t[7:8, :columns] + t[7:8, columns : 2 * columns] for t in terms], axis=0)
    power = jnp.concatenate([t[7:8, 2 * columns : 2 * columns + 1] + t[7:8, 2 * columns + 128 : 2 * columns + 129] for t in terms], axis=0)
    mean = jnp.sum(local, axis=0, keepdims=True) / 8
    apart = local - mean
    var = (jnp.sum(css, axis=0, keepdims=True) + (D // 8) * jnp.sum(apart * apart, axis=0, keepdims=True)) / D
    inv = lax.rsqrt(var + 1e-06)
    flat = jnp.concatenate([lean, apart, power * apart, apart, inv, mean, jnp.zeros((94, TOKENS), F32)], axis=0)
    turned[...] = flat.T
    mine = turned[pl.ds(pl.multiple_of(place * 16, 16), 16)]
    right = jnp.concatenate([apart, lean, apart], axis=0)
    gram = (gram + dot(mine[:, :24], right, ((1,), (0,)), exact)) * mine[:, 32:33] * inv
    rows[...] = gram.astype(BF)
    here = turned[pl.ds(pl.multiple_of(x * 256, 256), 256)]
    full[...] = total + dot(here[:, 24:32], column, ((1,), (0,)), exact)
    scales[...] = turned[...]


def stats_work(at, got, own, moved, cot, cot_other):
    columns = own.shape[1]
    vmem = pl.BlockSpec(memory_space=pltpu.VMEM)
    return pl.pallas_call(
        stats_kernel,
        out_shape=[
            jax.ShapeDtypeStruct((16, TOKENS), BF),
            jax.ShapeDtypeStruct((256, columns), BF),
            jax.ShapeDtypeStruct((256, columns), F32),
            jax.ShapeDtypeStruct((2, 128, columns), BF),
            jax.ShapeDtypeStruct((TOKENS, 128), F32),
        ],
        in_specs=[pl.BlockSpec(memory_space=pltpu.SMEM)] + [vmem] * 7,
        out_specs=[vmem] * 5,
        scratch_shapes=[pltpu.VMEM((TOKENS, 128), F32)],
        compiler_params=pltpu.CompilerParams(vmem_limit_bytes=40 << 20),
        cost_estimate=pl.CostEstimate(flops=10 << 20, bytes_accessed=3 << 20, transcendentals=0),
        name="stats_work",
    )(at, got, own, *moved, cot, cot_other)


def pre_kernel(at, full, moved, scales, one, two, three, out, mark):
    inv = scales[pl.ds(pl.multiple_of(at[2] * 256, 256), 256)][:, 32:33]
    out[...] = ((full[...] + moved[...].astype(F32)) * inv).astype(BF)
    mark[...] = inv[:8]


def pre_work(at, full, moved, scales, cots):
    vmem = pl.BlockSpec(memory_space=pltpu.VMEM)
    return pl.pallas_call(
        pre_kernel,
        out_shape=[jax.ShapeDtypeStruct(full.shape, BF), jax.ShapeDtypeStruct((8, 1), F32)],
        in_specs=[pl.BlockSpec(memory_space=pltpu.SMEM)] + [vmem] * 3 + [pl.BlockSpec(memory_space=pl.ANY)] * 3,
        out_specs=[vmem] * 2,
        compiler_params=pltpu.CompilerParams(vmem_limit_bytes=40 << 20),
        cost_estimate=pl.CostEstimate(flops=1 << 20, bytes_accessed=1 << 20, transcendentals=0),
        name="pre_work",
    )(at, full, moved, scales, *cots)


def slope_of(cot, value):
    return (cot.astype(F32) * gelu_slope(value) * (1.0 / math.sqrt(TOKENS))).astype(BF)


def ascent_kernel(at, mine, other, p0, p1, p2, p3, c0, c1, c2, c3, mark, along, pre_out, cot_out, squared, slope, pre, cot, sems):
    core, x = at[1], at[2]
    columns = p0.shape[1]
    for b, (p, c) in enumerate(((p0, c0), (p1, c1), (p2, c2), (p3, c3))):
        q = x ^ b
        pre[pl.ds(pl.multiple_of(q * 256, 256), 256)] = p[...]
        cot[pl.ds(pl.multiple_of(q * 128, 128), 128)] = c[0]
        cot[pl.ds(pl.multiple_of(512 + q * 128, 128), 128)] = c[1]
    copies = [pltpu.make_async_copy(pre, pre_out, sems.at[0]), pltpu.make_async_copy(cot, cot_out, sems.at[1])]
    for copy in copies:
        copy.start()
    for i in range(8):
        rows = pl.ds(128 * i, 128)
        value = slope_of(cot[rows], pre[rows].astype(F32))
        slope[pl.ds(4 * i, 4)] = value.reshape(4, 2, 16, columns)
    total = jnp.zeros((1, 1), F32)
    for gram, c in ((mine, core), (other, 1 - core)):
        for i in range(2):
            chips = pl.ds(16 * i, 16)
            part = dot(gram[chips].reshape(256, TOKENS), slope[...].reshape(TOKENS, columns), ((1,), (0,)))
            along[chips, c] = part.reshape(16, 16, columns)
            weighed = part * slope[chips, c].reshape(256, columns).astype(F32)
            total = total + jnp.sum(jnp.sum(weighed, axis=0, keepdims=True), axis=1, keepdims=True)
    squared[...] = jnp.broadcast_to(total.reshape(1, 1, 1), squared.shape)
    for copy in copies:
        copy.wait()


def ascent_work(at, mine, other, pres, cots, mark):
    columns = pres[0].shape[1]
    vmem = pl.BlockSpec(memory_space=pltpu.VMEM)
    anywhere = pl.BlockSpec(memory_space=pl.ANY)
    flat = jax.ShapeDtypeStruct((TOKENS, columns), BF)
    return pl.pallas_call(
        ascent_kernel,
        out_shape=[
            jax.ShapeDtypeStruct((32, 2, 16, columns), F32),
            flat,
            flat,
            jax.ShapeDtypeStruct((64, 1, 128), F32),
        ],
        in_specs=[pl.BlockSpec(memory_space=pltpu.SMEM)] + [vmem] * 10 + [anywhere],
        out_specs=[vmem, anywhere, anywhere, vmem],
        scratch_shapes=[
            pltpu.VMEM((32, 2, 16, columns), BF),
            pltpu.VMEM((TOKENS, columns), BF),
            pltpu.VMEM((TOKENS, columns), BF),
            pltpu.SemaphoreType.DMA((2,)),
        ],
        compiler_params=pltpu.CompilerParams(vmem_limit_bytes=40 << 20),
        cost_estimate=pl.CostEstimate(flops=2 * TOKENS * TOKENS * columns, bytes_accessed=8 << 20, transcendentals=2 * TOKENS * columns),
        name="ascent_work",
    )(at, mine, other, *pres, *cots, mark)


def per_device(tokens, norm_gain, w_up, cotangent):
    width, columns = w_up.shape
    places = (lax.axis_index(DP), lax.axis_index("c"), lax.axis_index("x"), lax.axis_index("yh"))
    at = jnp.stack(places).astype(jnp.int32)
    with jax.named_scope("token_gather"):
        mine = spread(tokens, ("yl", "z"), 32)
        mine, late = lax.optimization_barrier((mine, cotangent))
        other = swap(mine, "c", 1)
        cot_other = swap(late, "yh", 1)
    with jax.named_scope("local_work"):
        joined, own, near, opposite, far, sent = local_work(at, mine, other, norm_gain[None], w_up)
    with jax.named_scope("sums_x"):
        sent, cot_other = lax.optimization_barrier((sent, cot_other))
        got = spread(sent, MP, 8)
        moved = [swap(v, "x", b) for b, v in ((1, near), (2, opposite), (3, far))]
    with jax.named_scope("stats_work"):
        rows, half, full, pair, scales = stats_work(at, got, own, moved, cotangent, cot_other)
        normed = joined.reshape(TOKENS, width).astype(F32) - scales[:, 33:34]
        normed = (normed * scales[:, 32:33] * norm_gain[None, :]).astype(BF)
    with jax.named_scope("gram_gather"):
        gram = spread(rows, ("yl", "z"), 32)
    with jax.named_scope("pre"):
        moved = swap(half, "yh", 1)
        cots = gather_x(pair)
        pre, mark = pre_work(at, full, moved, scales, cots[1:])
        gram, mark = lax.optimization_barrier((gram, mark))
        pres = gather_x(pre)
        gram_other = swap(gram, "c", 1)
    with jax.named_scope("ascent"):
        along, pre, cot, squared = ascent_work(at, gram, gram_other, pres, cots, mark)
        squared = jnp.sum(lax.all_to_all(squared, DP, 0, 0, tiled=True)[:, 0, 0])
        size = jnp.sqrt(jnp.maximum(squared, 0.0)) + 1e-12
        radius = 0.5 * math.sqrt(FF)
    with jax.named_scope("sharp"):
        sharp = slope_of(cot, pre.astype(F32) + along.reshape(TOKENS, columns) * (radius / size))
        return dot(normed, sharp, ((0,), (0,)))


def solution(mesh):
    fine = Mesh(mesh.devices.reshape(4, 8, 2, 2, 4), DP + MP)
    placed = (P(DP, MP), P(MP), P(MP, DP), P(MP, DP))
    return jax.shard_map(
        per_device, mesh=fine, in_specs=placed, out_specs=P(MP, DP), check_vma=False
    )
```

```python
import math

import jax
import jax.numpy as jnp
from jax import lax
from jax.experimental import pallas as pl
from jax.experimental.pallas import tpu as pltpu
from jax.sharding import Mesh
from jax.sharding import PartitionSpec as P

FF = 24576
D = 6144
TOKENS = 1024
DP = ("yl", "z", "c")
MP = ("yh", "x")
BF = jnp.bfloat16
F32 = jnp.float32


def gelu_slope(value):
    cdf = 0.5 * (1.0 + lax.erf(value * (1.0 / math.sqrt(2.0))))
    dens = jnp.exp(-0.5 * value * value) * (1.0 / math.sqrt(2.0 * math.pi))
    return cdf + value * dens


def swap(value, axis, bit):
    size = lax.axis_size(axis)
    return lax.ppermute(value, axis, [(i, i ^ bit) for i in range(size)])


def spread(value, axes, count):
    copies = jnp.broadcast_to(value[None], (count,) + value.shape)
    return lax.all_to_all(copies, axes, 0, 0, tiled=True)


def gather_x(value):
    return [value] + [swap(value, "x", b) for b in (1, 2, 3)]


def dot(left, right, dims, precision=None):
    return lax.dot_general(left, right, (dims, ((), ())), precision=precision, preferred_element_type=F32)


def split(value, count):
    out = []
    for _ in range(count):
        out.append(value.astype(BF).astype(F32))
        value = value - out[-1]
    return out


def local_kernel(at, mine, other, gain, w, joined, own, near, opposite, far, sent, high, part, out, sems):
    place, core, x = at[0], at[1], at[2]
    g = gain[...]
    width = g.shape[1]
    ones = jnp.ones((8, width), BF)
    gains = jnp.concatenate(split(g, 3) + [jnp.zeros((5, width), F32)], axis=0).astype(BF)
    local, css, lean = [], [], []
    for i in range(8):
        chips = pl.ds(4 * i, 4)
        joined[chips, core] = mine[chips]
        joined[chips, 1 - core] = other[chips]
        raw = joined[chips].reshape(128, width)
        value = raw.astype(F32)
        centred = value - jnp.sum(value, axis=1, keepdims=True) * (1.0 / width)
        full = centred * g
        first = full.astype(BF)
        second = (full - first.astype(F32)).astype(BF)
        high[pl.ds(128 * i, 128)] = first
        rows = dot(first, w[...], ((1,), (0,))) + dot(second, w[...], ((1,), (0,)))
        part[i % 4, pl.ds(128 * (i // 4), 128)] = rows
        square = centred * centred
        top = square.astype(BF)
        rest = (square - top.astype(F32)).astype(BF)
        across = ((1,), (1,))
        local.append(dot(ones, raw, across)[:1] * (1.0 / width))
        css.append((dot(ones, top, across) + dot(ones, rest, across))[:1])
        lean.append(jnp.sum(dot(gains, first, across), axis=0, keepdims=True))
    own[...] = part[x]
    copies = []
    for b, target in ((1, near), (2, opposite), (3, far)):
        out[b - 1] = part[x ^ b].astype(BF)
        copies.append(pltpu.make_async_copy(out.at[b - 1], target, sems.at[b - 1]))
        copies[-1].start()
    gram = dot(high[pl.ds(pl.multiple_of(place * 16, 16), 16)], high[...], ((1,), (1,)))
    local, css, lean = (jnp.concatenate(v, axis=1) for v in (local, css, lean))
    column = jnp.sum(dot(gains, w[...], ((1,), (0,))), axis=0, keepdims=True)
    power = jnp.broadcast_to(jnp.sum(g * g, axis=1, keepdims=True), (1, 128))
    extra = jnp.concatenate(split(column, 2) + split(power, 2), axis=1)
    stats = jnp.concatenate(split(local, 3) + split(css, 2) + split(lean, 2) + [extra], axis=0)
    stats = [stats[:, 256 * q : 256 * q + 256] for q in range(4)]
    for j in range(8):
        q = 128 * (j % 4)
        block = jnp.concatenate([gram[:, q : q + 128], gram[:, 512 + q : 640 + q]], axis=1)
        sent[j] = jnp.concatenate([block] + stats, axis=0).astype(BF)
    for copy in copies:
        copy.wait()


def local_work(at, mine, other, gain, w):
    width, columns = w.shape
    block = jax.ShapeDtypeStruct((256, columns), BF)
    vmem = pl.BlockSpec(memory_space=pltpu.VMEM)
    return pl.pallas_call(
        local_kernel,
        out_shape=[
            jax.ShapeDtypeStruct((32, 2, 16, width), BF),
            jax.ShapeDtypeStruct((256, columns), F32),
            block,
            block,
            block,
            jax.ShapeDtypeStruct((8, 48, 256), BF),
        ],
        in_specs=[pl.BlockSpec(memory_space=pltpu.SMEM)] + [vmem] * 4,
        out_specs=[vmem] * 2 + [pl.BlockSpec(memory_space=pl.ANY)] * 3 + [vmem],
        scratch_shapes=[
            pltpu.VMEM((TOKENS, width), BF),
            pltpu.VMEM((4, 256, columns), F32),
            pltpu.VMEM((3, 256, columns), BF),
            pltpu.SemaphoreType.DMA((3,)),
        ],
        compiler_params=pltpu.CompilerParams(vmem_limit_bytes=40 << 20),
        cost_estimate=pl.CostEstimate(flops=2 * TOKENS * width * columns * 2, bytes_accessed=8 << 20, transcendentals=0),
        name="local_work",
    )(at, mine, other, gain, w)


def own_rows(ref, x):
    first = ref[pl.ds(pl.multiple_of(x * 128, 128), 128)]
    second = ref[pl.ds(pl.multiple_of(512 + x * 128, 128), 128)]
    return jnp.concatenate([first, second], axis=0)


def stats_kernel(at, got, own, one, two, three, cot, cot_other, rows, half, full, pair, scales, turned, wide):
    place, x = at[0], at[2]
    exact = lax.Precision.HIGHEST
    columns = own.shape[1]
    total = own[...] + one[...].astype(F32) + two[...].astype(F32) + three[...].astype(F32)
    half[...] = total.astype(BF)
    pair[at[3]] = cot[...]
    pair[1 - at[3]] = cot_other[...]
    gram = got[0, :16].astype(F32)
    for j in range(1, 8):
        gram = gram + got[j, :16].astype(F32)
    terms = [got[j, 16:].astype(F32) for j in range(8)]
    terms = [jnp.concatenate([t[8 * q : 8 * q + 8] for q in range(4)], axis=1) for t in terms]
    local = jnp.concatenate([t[0:1] + t[1:2] + t[2:3] for t in terms], axis=0)
    css = jnp.concatenate([t[3:4] + t[4:5] for t in terms], axis=0)
    lean = jnp.concatenate([t[5:6] + t[6:7] for t in terms], axis=0)
    column = jnp.concatenate([t[7:8, :columns] + t[7:8, columns : 2 * columns] for t in terms], axis=0)
    power = jnp.concatenate([t[7:8, 2 * columns : 2 * columns + 1] + t[7:8, 2 * columns + 128 : 2 * columns + 129] for t in terms], axis=0)
    mean = jnp.sum(local, axis=0, keepdims=True) / 8
    apart = local - mean
    var = (jnp.sum(css, axis=0, keepdims=True) + (D // 8) * jnp.sum(apart * apart, axis=0, keepdims=True)) / D
    inv = lax.rsqrt(var + 1e-06)
    flat = jnp.concatenate([lean, apart, power * apart, apart, inv, mean, jnp.zeros((94, TOKENS), F32)], axis=0)
    turned[...] = flat.T
    wide[...] = jnp.concatenate([apart, lean, apart, inv, jnp.zeros((7, TOKENS), F32)], axis=0)
    first = wide[:, pl.ds(pl.multiple_of(x * 128, 128), 128)]
    second = wide[:, pl.ds(pl.multiple_of(512 + x * 128, 128), 128)]
    right = jnp.concatenate([first, second], axis=1)
    mine = turned[pl.ds(pl.multiple_of(place * 16, 16), 16)]
    gram = (gram + dot(mine[:, :24], right[:24], ((1,), (0,)), exact)) * mine[:, 32:33] * right[24:25]
    rows[...] = gram.astype(BF)
    full[...] = total + dot(own_rows(turned, x)[:, 24:32], column, ((1,), (0,)), exact)
    scales[...] = turned[...]


def stats_work(at, got, own, moved, cot, cot_other):
    columns = own.shape[1]
    vmem = pl.BlockSpec(memory_space=pltpu.VMEM)
    return pl.pallas_call(
        stats_kernel,
        out_shape=[
            jax.ShapeDtypeStruct((16, 256), BF),
            jax.ShapeDtypeStruct((256, columns), BF),
            jax.ShapeDtypeStruct((256, columns), F32),
            jax.ShapeDtypeStruct((2, 128, columns), BF),
            jax.ShapeDtypeStruct((TOKENS, 128), F32),
        ],
        in_specs=[pl.BlockSpec(memory_space=pltpu.SMEM)] + [vmem] * 7,
        out_specs=[vmem] * 5,
        scratch_shapes=[pltpu.VMEM((TOKENS, 128), F32), pltpu.VMEM((32, TOKENS), F32)],
        compiler_params=pltpu.CompilerParams(vmem_limit_bytes=40 << 20),
        cost_estimate=pl.CostEstimate(flops=10 << 20, bytes_accessed=3 << 20, transcendentals=0),
        name="stats_work",
    )(at, got, own, *moved, cot, cot_other)


def slope_of(cot, value):
    return (cot.astype(F32) * gelu_slope(value) * (1.0 / math.sqrt(TOKENS))).astype(BF)


def slope_kernel(at, full, moved, scales, pair, pre, slope, mark):
    inv = own_rows(scales, at[2])[:, 32:33]
    value = (full[...] + moved[...].astype(F32)) * inv
    pre[...] = value
    slope[...] = slope_of(pair[...].reshape(value.shape), value)
    mark[...] = inv[:8]


def slope_work(at, full, moved, scales, pair):
    vmem = pl.BlockSpec(memory_space=pltpu.VMEM)
    return pl.pallas_call(
        slope_kernel,
        out_shape=[
            jax.ShapeDtypeStruct(full.shape, F32),
            jax.ShapeDtypeStruct(full.shape, BF),
            jax.ShapeDtypeStruct((8, 1), F32),
        ],
        in_specs=[pl.BlockSpec(memory_space=pltpu.SMEM)] + [vmem] * 4,
        out_specs=[vmem] * 3,
        compiler_params=pltpu.CompilerParams(vmem_limit_bytes=40 << 20),
        cost_estimate=pl.CostEstimate(flops=4 << 20, bytes_accessed=1 << 20, transcendentals=1 << 18),
        name="slope_work",
    )(at, full, moved, scales, pair)


def in_order(x, blocks, ordered):
    for b, block in enumerate(blocks):
        q = x ^ b
        shape = (4, 2, 16, block.shape[1])
        ordered[pl.ds(4 * q, 4)] = block[:128].reshape(shape)
        ordered[pl.ds(16 + 4 * q, 4)] = block[128:].reshape(shape)


def ascent_kernel(at, mine, other, s0, s1, s2, s3, mark, along, squared, ordered):
    core = at[1]
    columns = s0.shape[1]
    in_order(at[2], (s0, s1, s2, s3), ordered)
    half = TOKENS // 2
    part = dot(mine[...].reshape(half, 256), ordered[:, core].reshape(half, columns), ((0,), (0,)))
    part = part + dot(other[...].reshape(half, 256), ordered[:, 1 - core].reshape(half, columns), ((0,), (0,)))
    along[...] = part
    total = jnp.sum(jnp.sum(part * s0[...].astype(F32), axis=0, keepdims=True), axis=1, keepdims=True)
    squared[...] = jnp.broadcast_to(total.reshape(1, 1, 1), squared.shape)


def ascent_work(at, mine, other, slopes, mark):
    columns = slopes[0].shape[1]
    vmem = pl.BlockSpec(memory_space=pltpu.VMEM)
    return pl.pallas_call(
        ascent_kernel,
        out_shape=[jax.ShapeDtypeStruct((256, columns), F32), jax.ShapeDtypeStruct((256, 1, 128), F32)],
        in_specs=[pl.BlockSpec(memory_space=pltpu.SMEM)] + [vmem] * 6 + [pl.BlockSpec(memory_space=pl.ANY)],
        out_specs=[vmem] * 2,
        scratch_shapes=[pltpu.VMEM((32, 2, 16, columns), BF)],
        compiler_params=pltpu.CompilerParams(vmem_limit_bytes=40 << 20),
        cost_estimate=pl.CostEstimate(flops=2 * TOKENS * 256 * columns, bytes_accessed=2 << 20, transcendentals=0),
        name="ascent_work",
    )(at, mine, other, *slopes, mark)


def result_kernel(at, turned, s0, s1, s2, s3, out, ordered):
    in_order(at[2], (s0, s1, s2, s3), ordered)
    out[...] = dot(turned[...], ordered[...].reshape(TOKENS, out.shape[1]), ((1,), (0,)))


def result_work(at, turned, slopes):
    columns = slopes[0].shape[1]
    vmem = pl.BlockSpec(memory_space=pltpu.VMEM)
    return pl.pallas_call(
        result_kernel,
        out_shape=jax.ShapeDtypeStruct((turned.shape[0], columns), F32),
        in_specs=[pl.BlockSpec(memory_space=pltpu.SMEM)] + [vmem] * 5,
        out_specs=vmem,
        scratch_shapes=[pltpu.VMEM((32, 2, 16, columns), BF)],
        compiler_params=pltpu.CompilerParams(vmem_limit_bytes=40 << 20),
        cost_estimate=pl.CostEstimate(flops=2 * TOKENS * 768 * columns, bytes_accessed=4 << 20, transcendentals=0),
        name="result_work",
    )(at, turned, *slopes)


def per_device(tokens, norm_gain, w_up, cotangent):
    width = w_up.shape[0]
    places = (lax.axis_index(DP), lax.axis_index("c"), lax.axis_index("x"), lax.axis_index("yh"))
    at = jnp.stack(places).astype(jnp.int32)
    with jax.named_scope("token_gather"):
        mine = spread(tokens, ("yl", "z"), 32)
        mine, late = lax.optimization_barrier((mine, cotangent))
        other = swap(mine, "c", 1)
        cot_other = swap(late, "yh", 1)
    with jax.named_scope("local_work"):
        joined, own, near, opposite, far, sent = local_work(at, mine, other, norm_gain[None], w_up)
    with jax.named_scope("sums_x"):
        sent, cot_other = lax.optimization_barrier((sent, cot_other))
        got = lax.all_to_all(sent, MP, 0, 0, tiled=True)
        moved = [swap(v, "x", b) for b, v in ((1, near), (2, opposite), (3, far))]
    with jax.named_scope("stats_work"):
        rows, half, full, pair, scales = stats_work(at, got, own, moved, cotangent, cot_other)
        normed = joined.reshape(TOKENS, width).astype(F32) - scales[:, 33:34]
        turned = (normed * scales[:, 32:33] * norm_gain[None, :]).astype(BF).T
    with jax.named_scope("gram_gather"):
        gram = spread(rows, ("yl", "z"), 32)
    with jax.named_scope("slope"):
        moved = swap(half, "yh", 1)
        pre, slope, mark = slope_work(at, full, moved, scales, pair)
        gram, mark = lax.optimization_barrier((gram, mark))
        gram_other = swap(gram, "c", 1)
        slopes = gather_x(slope)
    with jax.named_scope("ascent"):
        along, squared = ascent_work(at, gram, gram_other, slopes, mark)
        squared = jnp.sum(lax.all_to_all(squared, DP + ("x",), 0, 0, tiled=True)[:, 0, 0])
        size = jnp.sqrt(jnp.maximum(squared, 0.0)) + 1e-12
        radius = 0.5 * math.sqrt(FF)
    with jax.named_scope("sharp"):
        sharp = slope_of(pair.reshape(pre.shape), pre + along * (radius / size))
        return result_work(at, turned, gather_x(sharp))


def solution(mesh):
    fine = Mesh(mesh.devices.reshape(4, 8, 2, 2, 4), DP + MP)
    placed = (P(DP, MP), P(MP), P(MP, DP), P(MP, DP))
    return jax.shard_map(
        per_device, mesh=fine, in_specs=placed, out_specs=P(MP, DP), check_vma=False
    )
```

```python
import math

import jax
import jax.numpy as jnp
from jax import lax
from jax.experimental import pallas as pl
from jax.experimental.pallas import tpu as pltpu
from jax.sharding import Mesh
from jax.sharding import PartitionSpec as P

FF = 24576
D = 6144
TOKENS = 1024
DP = ("yl", "z", "c")
MP = ("yh", "x")
BF = jnp.bfloat16
F32 = jnp.float32


def gelu_slope(value):
    cdf = 0.5 * (1.0 + lax.erf(value * (1.0 / math.sqrt(2.0))))
    dens = jnp.exp(-0.5 * value * value) * (1.0 / math.sqrt(2.0 * math.pi))
    return cdf + value * dens


def swap(value, axis, bit):
    size = lax.axis_size(axis)
    return lax.ppermute(value, axis, [(i, i ^ bit) for i in range(size)])


def spread(value, axes, count):
    copies = jnp.broadcast_to(value[None], (count,) + value.shape)
    return lax.all_to_all(copies, axes, 0, 0, tiled=True)


def gather_x(value):
    return [value] + [swap(value, "x", b) for b in (1, 2, 3)]


def dot(left, right, dims, precision=None):
    return lax.dot_general(left, right, (dims, ((), ())), precision=precision, preferred_element_type=F32)


def split(value, count):
    out = []
    for _ in range(count):
        out.append(value.astype(BF).astype(F32))
        value = value - out[-1]
    return out


def fetch(sources, targets, sems):
    copies = [pltpu.make_async_copy(s, t, sems.at[i]) for i, (s, t) in enumerate(zip(sources, targets))]
    for copy in copies:
        copy.start()
    return copies


HBM = pl.BlockSpec(memory_space=pltpu.HBM)


def local_kernel(at, mine, other, gain, w_far, joined, own, near, opposite, far, sent, high, part, out, w, sems, in_sems):
    place, core, x = at[0], at[1], at[2]
    halves = [pl.ds(16 * i, 16) for i in range(2)]
    sources = [v.at[h] for h in halves for v in (mine, other)]
    targets = [joined.at[h, c] for h in halves for c in (core, 1 - core)]
    arrivals = fetch(sources[:2] + [w_far] + sources[2:], targets[:2] + [w] + targets[2:], in_sems)
    g = gain[...]
    width = g.shape[1]
    ones = jnp.ones((8, width), BF)
    gains = jnp.concatenate(split(g, 3) + [jnp.zeros((5, width), F32)], axis=0).astype(BF)
    local, css, lean = [], [], []
    for i in range(8):
        chips = pl.ds(4 * i, 4)
        for copy in {0: arrivals[:3], 4: arrivals[3:]}.get(i, []):
            copy.wait()
        raw = joined[chips].reshape(128, width)
        value = raw.astype(F32)
        centred = value - jnp.sum(value, axis=1, keepdims=True) * (1.0 / width)
        full = centred * g
        first = full.astype(BF)
        second = (full - first.astype(F32)).astype(BF)
        high[pl.ds(128 * i, 128)] = first
        rows = dot(first, w[...], ((1,), (0,))) + dot(second, w[...], ((1,), (0,)))
        part[i % 4, pl.ds(128 * (i // 4), 128)] = rows
        square = centred * centred
        top = square.astype(BF)
        rest = (square - top.astype(F32)).astype(BF)
        across = ((1,), (1,))
        local.append(dot(ones, raw, across)[:1] * (1.0 / width))
        css.append((dot(ones, top, across) + dot(ones, rest, across))[:1])
        lean.append(jnp.sum(dot(gains, first, across), axis=0, keepdims=True))
    own[...] = part[x]
    copies = []
    for b, target in ((1, near), (2, opposite), (3, far)):
        out[b - 1] = part[x ^ b].astype(BF)
        copies.append(pltpu.make_async_copy(out.at[b - 1], target, sems.at[b - 1]))
        copies[-1].start()
    gram = dot(high[pl.ds(pl.multiple_of(place * 16, 16), 16)], high[...], ((1,), (1,)))
    local, css, lean = (jnp.concatenate(v, axis=1) for v in (local, css, lean))
    column = jnp.sum(dot(gains, w[...], ((1,), (0,))), axis=0, keepdims=True)
    power = jnp.broadcast_to(jnp.sum(g * g, axis=1, keepdims=True), (1, 128))
    extra = jnp.concatenate(split(column, 2) + split(power, 2), axis=1)
    stats = jnp.concatenate(split(local, 3) + split(css, 2) + split(lean, 2) + [extra], axis=0)
    stats = [stats[:, 256 * q : 256 * q + 256] for q in range(4)]
    for j in range(8):
        q = 128 * (j % 4)
        block = jnp.concatenate([gram[:, q : q + 128], gram[:, 512 + q : 640 + q]], axis=1)
        sent[j] = jnp.concatenate([block] + stats, axis=0).astype(BF)
    for copy in copies:
        copy.wait()


def local_work(at, mine, other, gain, w):
    width, columns = w.shape
    block = jax.ShapeDtypeStruct((256, columns), BF)
    vmem = pl.BlockSpec(memory_space=pltpu.VMEM)
    return pl.pallas_call(
        local_kernel,
        out_shape=[
            jax.ShapeDtypeStruct((32, 2, 16, width), BF),
            jax.ShapeDtypeStruct((256, columns), F32),
            block,
            block,
            block,
            jax.ShapeDtypeStruct((8, 48, 256), BF),
        ],
        in_specs=[pl.BlockSpec(memory_space=pltpu.SMEM), HBM, HBM, vmem, HBM],
        out_specs=[vmem] * 2 + [HBM] * 3 + [vmem],
        scratch_shapes=[
            pltpu.VMEM((TOKENS, width), BF),
            pltpu.VMEM((4, 256, columns), F32),
            pltpu.VMEM((3, 256, columns), BF),
            pltpu.VMEM((width, columns), BF),
            pltpu.SemaphoreType.DMA((3,)),
            pltpu.SemaphoreType.DMA((5,)),
        ],
        compiler_params=pltpu.CompilerParams(vmem_limit_bytes=40 << 20),
        cost_estimate=pl.CostEstimate(flops=2 * TOKENS * width * columns * 2, bytes_accessed=8 << 20, transcendentals=0),
        name="local_work",
    )(at, mine, other, gain, w)


def own_rows(ref, x):
    first = ref[pl.ds(pl.multiple_of(x * 128, 128), 128)]
    second = ref[pl.ds(pl.multiple_of(512 + x * 128, 128), 128)]
    return jnp.concatenate([first, second], axis=0)


def stats_kernel(
    at, got_far, own, one_far, two_far, three_far, cot, cot_other_far, rows, half_far, full_far, pair, scales,
    turned, wide, got, one, two, three, cot_other, half, full, sems,
):
    place, x = at[0], at[2]
    exact = lax.Precision.HIGHEST
    columns = own.shape[1]
    sources = (one_far, two_far, three_far, got_far, cot_other_far)
    for copy in fetch(sources, (one, two, three, got, cot_other), sems):
        copy.wait()
    total = own[...] + one[...].astype(F32) + two[...].astype(F32) + three[...].astype(F32)
    half[...] = total.astype(BF)
    away = fetch((half,), (half_far,), sems.at[pl.ds(5, 1)])
    pair[at[3]] = cot[...]
    pair[1 - at[3]] = cot_other[...]
    gram = got[0, :16].astype(F32)
    for j in range(1, 8):
        gram = gram + got[j, :16].astype(F32)
    terms = [got[j, 16:].astype(F32) for j in range(8)]
    terms = [jnp.concatenate([t[8 * q : 8 * q + 8] for q in range(4)], axis=1) for t in terms]
    local = jnp.concatenate([t[0:1] + t[1:2] + t[2:3] for t in terms], axis=0)
    css = jnp.concatenate([t[3:4] + t[4:5] for t in terms], axis=0)
    lean = jnp.concatenate([t[5:6] + t[6:7] for t in terms], axis=0)
    column = jnp.concatenate([t[7:8, :columns] + t[7:8, columns : 2 * columns] for t in terms], axis=0)
    power = jnp.concatenate([t[7:8, 2 * columns : 2 * columns + 1] + t[7:8, 2 * columns + 128 : 2 * columns + 129] for t in terms], axis=0)
    mean = jnp.sum(local, axis=0, keepdims=True) / 8
    apart = local - mean
    var = (jnp.sum(css, axis=0, keepdims=True) + (D // 8) * jnp.sum(apart * apart, axis=0, keepdims=True)) / D
    inv = lax.rsqrt(var + 1e-06)
    flat = jnp.concatenate([lean, apart, power * apart, apart, inv, mean, jnp.zeros((94, TOKENS), F32)], axis=0)
    turned[...] = flat.T
    wide[...] = jnp.concatenate([apart, lean, apart, inv, jnp.zeros((7, TOKENS), F32)], axis=0)
    first = wide[:, pl.ds(pl.multiple_of(x * 128, 128), 128)]
    second = wide[:, pl.ds(pl.multiple_of(512 + x * 128, 128), 128)]
    right = jnp.concatenate([first, second], axis=1)
    mine = turned[pl.ds(pl.multiple_of(place * 16, 16), 16)]
    gram = (gram + dot(mine[:, :24], right[:24], ((1,), (0,)), exact)) * mine[:, 32:33] * right[24:25]
    rows[...] = gram.astype(BF)
    full[...] = total + dot(own_rows(turned, x)[:, 24:32], column, ((1,), (0,)), exact)
    away += fetch((full,), (full_far,), sems.at[pl.ds(6, 1)])
    scales[...] = turned[...]
    for copy in away:
        copy.wait()


def stats_work(at, got, own, moved, cot, cot_other):
    columns = own.shape[1]
    vmem = pl.BlockSpec(memory_space=pltpu.VMEM)
    return pl.pallas_call(
        stats_kernel,
        out_shape=[
            jax.ShapeDtypeStruct((16, 256), BF),
            jax.ShapeDtypeStruct((256, columns), BF),
            jax.ShapeDtypeStruct((256, columns), F32),
            jax.ShapeDtypeStruct((2, 128, columns), BF),
            jax.ShapeDtypeStruct((TOKENS, 128), F32),
        ],
        in_specs=[pl.BlockSpec(memory_space=pltpu.SMEM), HBM, vmem, HBM, HBM, HBM, vmem, HBM],
        out_specs=[vmem, HBM, HBM, vmem, vmem],
        scratch_shapes=[
            pltpu.VMEM((TOKENS, 128), F32),
            pltpu.VMEM((32, TOKENS), F32),
            pltpu.VMEM(got.shape, BF),
            pltpu.VMEM((256, columns), BF),
            pltpu.VMEM((256, columns), BF),
            pltpu.VMEM((256, columns), BF),
            pltpu.VMEM((128, columns), BF),
            pltpu.VMEM((256, columns), BF),
            pltpu.VMEM((256, columns), F32),
            pltpu.SemaphoreType.DMA((7,)),
        ],
        compiler_params=pltpu.CompilerParams(vmem_limit_bytes=40 << 20),
        cost_estimate=pl.CostEstimate(flops=10 << 20, bytes_accessed=3 << 20, transcendentals=0),
        name="stats_work",
    )(at, got, own, *moved, cot, cot_other)


def slope_of(cot, value):
    return (cot.astype(F32) * gelu_slope(value) * (1.0 / math.sqrt(TOKENS))).astype(BF)


def slope_kernel(at, full_far, moved_far, scales, pair, turned, pre, slope_far, mark, full, moved, slope, sems):
    for copy in fetch((full_far, moved_far), (full, moved), sems):
        copy.wait()
    inv = own_rows(scales, at[2])[:, 32:33]
    value = (full[...] + moved[...].astype(F32)) * inv
    pre[...] = value
    slope[...] = slope_of(pair[...].reshape(value.shape), value)
    mark[...] = inv[:8]
    fetch((slope,), (slope_far,), sems.at[pl.ds(2, 1)])[0].wait()


def slope_work(at, full, moved, scales, pair, turned):
    vmem = pl.BlockSpec(memory_space=pltpu.VMEM)
    return pl.pallas_call(
        slope_kernel,
        out_shape=[
            jax.ShapeDtypeStruct(full.shape, F32),
            jax.ShapeDtypeStruct(full.shape, BF),
            jax.ShapeDtypeStruct((8, 1), F32),
        ],
        in_specs=[pl.BlockSpec(memory_space=pltpu.SMEM), HBM, HBM, vmem, vmem, HBM],
        out_specs=[vmem, HBM, vmem],
        scratch_shapes=[
            pltpu.VMEM(full.shape, F32),
            pltpu.VMEM(full.shape, BF),
            pltpu.VMEM(full.shape, BF),
            pltpu.SemaphoreType.DMA((3,)),
        ],
        compiler_params=pltpu.CompilerParams(vmem_limit_bytes=40 << 20),
        cost_estimate=pl.CostEstimate(flops=4 << 20, bytes_accessed=1 << 20, transcendentals=1 << 18),
        name="slope_work",
    )(at, full, moved, scales, pair, turned)


def norm_kernel(joined, scales, gain, turned):
    width = gain.shape[1]
    for i in range(8):
        rows = pl.ds(128 * i, 128)
        value = joined[pl.ds(4 * i, 4)].reshape(128, width).astype(F32) - scales[rows, 33:34]
        value = value * scales[rows, 32:33] * gain[...]
        turned[:, rows] = value.T.astype(BF)


def norm_work(joined, scales, gain):
    width = gain.shape[1]
    vmem = pl.BlockSpec(memory_space=pltpu.VMEM)
    return pl.pallas_call(
        norm_kernel,
        out_shape=jax.ShapeDtypeStruct((width, TOKENS), BF),
        in_specs=[vmem] * 3,
        out_specs=vmem,
        compiler_params=pltpu.CompilerParams(vmem_limit_bytes=40 << 20),
        cost_estimate=pl.CostEstimate(flops=4 << 20, bytes_accessed=4 << 20, transcendentals=0),
        name="norm_work",
    )(joined, scales, gain)


def in_order(x, blocks, ordered):
    for b, block in enumerate(blocks):
        q = x ^ b
        shape = (4, 2, 16, block.shape[1])
        ordered[pl.ds(4 * q, 4)] = block[:128].reshape(shape)
        ordered[pl.ds(16 + 4 * q, 4)] = block[128:].reshape(shape)


def ascent_kernel(at, mine, other, s0, s1, s2, s3, mark, along, squared, ordered):
    core = at[1]
    columns = s0.shape[1]
    in_order(at[2], (s0, s1, s2, s3), ordered)
    half = TOKENS // 2
    part = dot(mine[...].reshape(half, 256), ordered[:, core].reshape(half, columns), ((0,), (0,)))
    part = part + dot(other[...].reshape(half, 256), ordered[:, 1 - core].reshape(half, columns), ((0,), (0,)))
    along[...] = part
    total = jnp.sum(jnp.sum(part * s0[...].astype(F32), axis=0, keepdims=True), axis=1, keepdims=True)
    squared[...] = jnp.broadcast_to(total, squared.shape)


def ascent_work(at, mine, other, slopes, mark):
    columns = slopes[0].shape[1]
    vmem = pl.BlockSpec(memory_space=pltpu.VMEM)
    return pl.pallas_call(
        ascent_kernel,
        out_shape=[jax.ShapeDtypeStruct((256, columns), F32), jax.ShapeDtypeStruct((8, 128), F32)],
        in_specs=[pl.BlockSpec(memory_space=pltpu.SMEM)] + [vmem] * 6 + [pl.BlockSpec(memory_space=pl.ANY)],
        out_specs=[vmem] * 2,
        scratch_shapes=[pltpu.VMEM((32, 2, 16, columns), BF)],
        compiler_params=pltpu.CompilerParams(vmem_limit_bytes=40 << 20),
        cost_estimate=pl.CostEstimate(flops=2 * TOKENS * 256 * columns, bytes_accessed=2 << 20, transcendentals=0),
        name="ascent_work",
    )(at, mine, other, *slopes, mark)


def result_kernel(at, turned, s0, s1, s2, s3, out, ordered):
    in_order(at[2], (s0, s1, s2, s3), ordered)
    out[...] = dot(turned[...], ordered[...].reshape(TOKENS, out.shape[1]), ((1,), (0,)))


def result_work(at, turned, slopes):
    columns = slopes[0].shape[1]
    vmem = pl.BlockSpec(memory_space=pltpu.VMEM)
    return pl.pallas_call(
        result_kernel,
        out_shape=jax.ShapeDtypeStruct((turned.shape[0], columns), F32),
        in_specs=[pl.BlockSpec(memory_space=pltpu.SMEM)] + [vmem] * 5,
        out_specs=vmem,
        scratch_shapes=[pltpu.VMEM((32, 2, 16, columns), BF)],
        compiler_params=pltpu.CompilerParams(vmem_limit_bytes=40 << 20),
        cost_estimate=pl.CostEstimate(flops=2 * TOKENS * 768 * columns, bytes_accessed=4 << 20, transcendentals=0),
        name="result_work",
    )(at, turned, *slopes)


def per_device(tokens, norm_gain, w_up, cotangent):
    width = w_up.shape[0]
    places = (lax.axis_index(DP), lax.axis_index("c"), lax.axis_index("x"), lax.axis_index("yh"))
    at = jnp.stack(places).astype(jnp.int32)
    with jax.named_scope("token_gather"):
        mine = spread(tokens, ("yl", "z"), 32)
        mine, late = lax.optimization_barrier((mine, cotangent))
        other = swap(mine, "c", 1)
        cot_other = swap(late, "yh", 1)
    with jax.named_scope("local_work"):
        joined, own, near, opposite, far, sent = local_work(at, mine, other, norm_gain[None], w_up)
    with jax.named_scope("sums_x"):
        sent, cot_other = lax.optimization_barrier((sent, cot_other))
        got = lax.all_to_all(sent, MP, 0, 0, tiled=True)
        moved = [swap(v, "x", b) for b, v in ((1, near), (2, opposite), (3, far))]
    with jax.named_scope("stats_work"):
        rows, half, full, pair, scales = stats_work(at, got, own, moved, cotangent, cot_other)
        turned = norm_work(joined, scales, norm_gain[None])
    with jax.named_scope("gram_gather"):
        gram = spread(rows, ("yl", "z"), 32)
    with jax.named_scope("slope"):
        moved = swap(half, "yh", 1)
        pre, slope, mark = slope_work(at, full, moved, scales, pair, turned)
        gram, mark = lax.optimization_barrier((gram, mark))
        gram_other = swap(gram, "c", 1)
        slopes = gather_x(slope)
    with jax.named_scope("ascent"):
        along, squared = ascent_work(at, gram, gram_other, slopes, mark)
        squared = sum(gather_x(squared))[:1]
        squared = jnp.sum(spread(squared, DP, 64)[:, 0, 0])
        size = jnp.sqrt(jnp.maximum(squared, 0.0)) + 1e-12
        radius = 0.5 * math.sqrt(FF)
    with jax.named_scope("sharp"):
        sharp = slope_of(pair.reshape(pre.shape), pre + along * (radius / size))
        return result_work(at, turned, gather_x(sharp))


def solution(mesh):
    fine = Mesh(mesh.devices.reshape(4, 8, 2, 2, 4), DP + MP)
    placed = (P(DP, MP), P(MP), P(MP, DP), P(MP, DP))
    return jax.shard_map(
        per_device, mesh=fine, in_specs=placed, out_specs=P(MP, DP), check_vma=False
    )
```

```python
import math

import jax
import jax.numpy as jnp
from jax import lax
from jax.experimental import pallas as pl
from jax.experimental.pallas import tpu as pltpu
from jax.sharding import Mesh
from jax.sharding import PartitionSpec as P

FF = 24576
D = 6144
TOKENS = 1024
DP = ("yl", "z", "c")
MP = ("yh", "x")
BF = jnp.bfloat16
F32 = jnp.float32


def gelu_slope(value):
    cdf = 0.5 * (1.0 + lax.erf(value * (1.0 / math.sqrt(2.0))))
    dens = jnp.exp(-0.5 * value * value) * (1.0 / math.sqrt(2.0 * math.pi))
    return cdf + value * dens


def swap(value, axis, bit):
    size = lax.axis_size(axis)
    return lax.ppermute(value, axis, [(i, i ^ bit) for i in range(size)])


def spread(value, axes, count):
    copies = jnp.broadcast_to(value[None], (count,) + value.shape)
    return lax.all_to_all(copies, axes, 0, 0, tiled=True)


def gather_x(value):
    return [value] + [swap(value, "x", b) for b in (1, 2, 3)]


def dot(left, right, dims, precision=None):
    return lax.dot_general(left, right, (dims, ((), ())), precision=precision, preferred_element_type=F32)


def split(value, count):
    out = []
    for _ in range(count):
        out.append(value.astype(BF).astype(F32))
        value = value - out[-1]
    return out


def fetch(sources, targets, sems):
    copies = [pltpu.make_async_copy(s, t, sems.at[i]) for i, (s, t) in enumerate(zip(sources, targets))]
    for copy in copies:
        copy.start()
    return copies


HBM = pl.BlockSpec(memory_space=pltpu.HBM)


def local_kernel(at, mine, other, gain, w_far, joined, own, near, opposite, far, sent, high, part, out, w, sems, in_sems):
    place, core, x = at[0], at[1], at[2]
    halves = [pl.ds(16 * i, 16) for i in range(2)]
    sources = [v.at[h] for h in halves for v in (mine, other)]
    targets = [joined.at[h, c] for h in halves for c in (core, 1 - core)]
    arrivals = fetch(sources[:2] + [w_far] + sources[2:], targets[:2] + [w] + targets[2:], in_sems)
    g = gain[...]
    width = g.shape[1]
    ones = jnp.ones((8, width), BF)
    gains = jnp.concatenate(split(g, 3) + [jnp.zeros((5, width), F32)], axis=0).astype(BF)
    local, css, lean = [], [], []
    for i in range(8):
        chips = pl.ds(4 * i, 4)
        for copy in {0: arrivals[:3], 4: arrivals[3:]}.get(i, []):
            copy.wait()
        raw = joined[chips].reshape(128, width)
        value = raw.astype(F32)
        centred = value - jnp.sum(value, axis=1, keepdims=True) * (1.0 / width)
        full = centred * g
        first = full.astype(BF)
        second = (full - first.astype(F32)).astype(BF)
        high[pl.ds(128 * i, 128)] = first
        rows = dot(first, w[...], ((1,), (0,))) + dot(second, w[...], ((1,), (0,)))
        part[i % 4, pl.ds(128 * (i // 4), 128)] = rows
        square = centred * centred
        top = square.astype(BF)
        rest = (square - top.astype(F32)).astype(BF)
        across = ((1,), (1,))
        local.append(dot(ones, raw, across)[:1] * (1.0 / width))
        css.append((dot(ones, top, across) + dot(ones, rest, across))[:1])
        lean.append(jnp.sum(dot(gains, first, across), axis=0, keepdims=True))
    own[...] = part[x]
    copies = []
    for b, target in ((1, near), (2, opposite), (3, far)):
        out[b - 1] = part[x ^ b].astype(BF)
        copies.append(pltpu.make_async_copy(out.at[b - 1], target, sems.at[b - 1]))
        copies[-1].start()
    gram = dot(high[pl.ds(pl.multiple_of(place * 16, 16), 16)], high[...], ((1,), (1,)))
    local, css, lean = (jnp.concatenate(v, axis=1) for v in (local, css, lean))
    column = jnp.sum(dot(gains, w[...], ((1,), (0,))), axis=0, keepdims=True)
    power = jnp.broadcast_to(jnp.sum(g * g, axis=1, keepdims=True), (1, 128))
    extra = jnp.concatenate(split(column, 2) + split(power, 2), axis=1)
    stats = jnp.concatenate(split(local, 3) + split(css, 2) + split(lean, 2) + [extra], axis=0)
    stats = [stats[:, 256 * q : 256 * q + 256] for q in range(4)]
    for j in range(8):
        q = 128 * (j % 4)
        block = jnp.concatenate([gram[:, q : q + 128], gram[:, 512 + q : 640 + q]], axis=1)
        sent[j] = jnp.concatenate(split(block, 2) + stats, axis=0).astype(BF)
    for copy in copies:
        copy.wait()


def local_work(at, mine, other, gain, w):
    width, columns = w.shape
    block = jax.ShapeDtypeStruct((256, columns), BF)
    vmem = pl.BlockSpec(memory_space=pltpu.VMEM)
    return pl.pallas_call(
        local_kernel,
        out_shape=[
            jax.ShapeDtypeStruct((32, 2, 16, width), BF),
            jax.ShapeDtypeStruct((256, columns), F32),
            block,
            block,
            block,
            jax.ShapeDtypeStruct((8, 64, 256), BF),
        ],
        in_specs=[pl.BlockSpec(memory_space=pltpu.SMEM), HBM, HBM, vmem, HBM],
        out_specs=[vmem] * 2 + [HBM] * 3 + [vmem],
        scratch_shapes=[
            pltpu.VMEM((TOKENS, width), BF),
            pltpu.VMEM((4, 256, columns), F32),
            pltpu.VMEM((3, 256, columns), BF),
            pltpu.VMEM((width, columns), BF),
            pltpu.SemaphoreType.DMA((3,)),
            pltpu.SemaphoreType.DMA((5,)),
        ],
        compiler_params=pltpu.CompilerParams(vmem_limit_bytes=40 << 20),
        cost_estimate=pl.CostEstimate(flops=2 * TOKENS * width * columns * 2, bytes_accessed=8 << 20, transcendentals=0),
        name="local_work",
    )(at, mine, other, gain, w)


def own_rows(ref, x):
    first = ref[pl.ds(pl.multiple_of(x * 128, 128), 128)]
    second = ref[pl.ds(pl.multiple_of(512 + x * 128, 128), 128)]
    return jnp.concatenate([first, second], axis=0)


def stats_kernel(
    at, got_far, own, one_far, two_far, three_far, cot, cot_other_far, rows, half_far, full_far, pair, scales,
    turned, wide, got, one, two, three, cot_other, half, full, sems,
):
    place, x = at[0], at[2]
    exact = lax.Precision.HIGHEST
    columns = own.shape[1]
    sources = (one_far, two_far, three_far, got_far, cot_other_far)
    for copy in fetch(sources, (one, two, three, got, cot_other), sems):
        copy.wait()
    total = own[...] + one[...].astype(F32) + two[...].astype(F32) + three[...].astype(F32)
    half[...] = total.astype(BF)
    away = fetch((half,), (half_far,), sems.at[pl.ds(5, 1)])
    pair[at[3]] = cot[...]
    pair[1 - at[3]] = cot_other[...]
    gram = jnp.zeros((16, 256), F32)
    for j in range(8):
        gram = gram + (got[j, :16].astype(F32) + got[j, 16:32].astype(F32))
    terms = [got[j, 32:].astype(F32) for j in range(8)]
    terms = [jnp.concatenate([t[8 * q : 8 * q + 8] for q in range(4)], axis=1) for t in terms]
    local = jnp.concatenate([t[0:1] + t[1:2] + t[2:3] for t in terms], axis=0)
    css = jnp.concatenate([t[3:4] + t[4:5] for t in terms], axis=0)
    lean = jnp.concatenate([t[5:6] + t[6:7] for t in terms], axis=0)
    column = jnp.concatenate([t[7:8, :columns] + t[7:8, columns : 2 * columns] for t in terms], axis=0)
    power = jnp.concatenate([t[7:8, 2 * columns : 2 * columns + 1] + t[7:8, 2 * columns + 128 : 2 * columns + 129] for t in terms], axis=0)
    mean = jnp.sum(local, axis=0, keepdims=True) / 8
    apart = local - mean
    var = (jnp.sum(css, axis=0, keepdims=True) + (D // 8) * jnp.sum(apart * apart, axis=0, keepdims=True)) / D
    inv = lax.rsqrt(var + 1e-06)
    flat = jnp.concatenate([lean, apart, power * apart, apart, inv, mean, jnp.zeros((94, TOKENS), F32)], axis=0)
    turned[...] = flat.T
    wide[...] = jnp.concatenate([apart, lean, apart, inv, jnp.zeros((7, TOKENS), F32)], axis=0)
    first = wide[:, pl.ds(pl.multiple_of(x * 128, 128), 128)]
    second = wide[:, pl.ds(pl.multiple_of(512 + x * 128, 128), 128)]
    right = jnp.concatenate([first, second], axis=1)
    mine = turned[pl.ds(pl.multiple_of(place * 16, 16), 16)]
    gram = (gram + dot(mine[:, :24], right[:24], ((1,), (0,)), exact)) * mine[:, 32:33] * right[24:25]
    for i, term in enumerate(split(gram, 2)):
        rows[i] = term.astype(BF)
    full[...] = total + dot(own_rows(turned, x)[:, 24:32], column, ((1,), (0,)), exact)
    away += fetch((full,), (full_far,), sems.at[pl.ds(6, 1)])
    scales[...] = turned[...]
    for copy in away:
        copy.wait()


def stats_work(at, got, own, moved, cot, cot_other):
    columns = own.shape[1]
    vmem = pl.BlockSpec(memory_space=pltpu.VMEM)
    return pl.pallas_call(
        stats_kernel,
        out_shape=[
            jax.ShapeDtypeStruct((2, 16, 256), BF),
            jax.ShapeDtypeStruct((256, columns), BF),
            jax.ShapeDtypeStruct((256, columns), F32),
            jax.ShapeDtypeStruct((2, 128, columns), BF),
            jax.ShapeDtypeStruct((TOKENS, 128), F32),
        ],
        in_specs=[pl.BlockSpec(memory_space=pltpu.SMEM), HBM, vmem, HBM, HBM, HBM, vmem, HBM],
        out_specs=[vmem, HBM, HBM, vmem, vmem],
        scratch_shapes=[
            pltpu.VMEM((TOKENS, 128), F32),
            pltpu.VMEM((32, TOKENS), F32),
            pltpu.VMEM(got.shape, BF),
            pltpu.VMEM((256, columns), BF),
            pltpu.VMEM((256, columns), BF),
            pltpu.VMEM((256, columns), BF),
            pltpu.VMEM((128, columns), BF),
            pltpu.VMEM((256, columns), BF),
            pltpu.VMEM((256, columns), F32),
            pltpu.SemaphoreType.DMA((7,)),
        ],
        compiler_params=pltpu.CompilerParams(vmem_limit_bytes=40 << 20),
        cost_estimate=pl.CostEstimate(flops=10 << 20, bytes_accessed=3 << 20, transcendentals=0),
        name="stats_work",
    )(at, got, own, *moved, cot, cot_other)


def slope_of(cot, value):
    return (cot.astype(F32) * gelu_slope(value) * (1.0 / math.sqrt(TOKENS))).astype(BF)


def pre_kernel(at, full_far, moved_far, scales, turned, one, two, three, out_far, mark, full, moved, out, sems):
    for copy in fetch((full_far, moved_far), (full, moved), sems):
        copy.wait()
    inv = own_rows(scales, at[2])[:, 32:33]
    out[...] = ((full[...] + moved[...].astype(F32)) * inv).astype(BF)
    mark[...] = inv[:8]
    fetch((out,), (out_far,), sems.at[pl.ds(2, 1)])[0].wait()


def pre_work(at, full, moved, scales, turned, cots):
    vmem = pl.BlockSpec(memory_space=pltpu.VMEM)
    return pl.pallas_call(
        pre_kernel,
        out_shape=[jax.ShapeDtypeStruct(full.shape, BF), jax.ShapeDtypeStruct((8, 1), F32)],
        in_specs=[pl.BlockSpec(memory_space=pltpu.SMEM), HBM, HBM, vmem] + [HBM] * 4,
        out_specs=[HBM, vmem],
        scratch_shapes=[
            pltpu.VMEM(full.shape, F32),
            pltpu.VMEM(full.shape, BF),
            pltpu.VMEM(full.shape, BF),
            pltpu.SemaphoreType.DMA((3,)),
        ],
        compiler_params=pltpu.CompilerParams(vmem_limit_bytes=40 << 20),
        cost_estimate=pl.CostEstimate(flops=1 << 20, bytes_accessed=1 << 20, transcendentals=0),
        name="pre_work",
    )(at, full, moved, scales, turned, *cots)


def norm_kernel(joined, scales, gain, turned):
    width = gain.shape[1]
    for i in range(8):
        rows = pl.ds(128 * i, 128)
        value = joined[pl.ds(4 * i, 4)].reshape(128, width).astype(F32) - scales[rows, 33:34]
        value = value * scales[rows, 32:33] * gain[...]
        turned[:, rows] = value.T.astype(BF)


def norm_work(joined, scales, gain):
    width = gain.shape[1]
    vmem = pl.BlockSpec(memory_space=pltpu.VMEM)
    return pl.pallas_call(
        norm_kernel,
        out_shape=jax.ShapeDtypeStruct((width, TOKENS), BF),
        in_specs=[vmem] * 3,
        out_specs=vmem,
        compiler_params=pltpu.CompilerParams(vmem_limit_bytes=40 << 20),
        cost_estimate=pl.CostEstimate(flops=4 << 20, bytes_accessed=4 << 20, transcendentals=0),
        name="norm_work",
    )(joined, scales, gain)


def put(q, block, ordered):
    shape = (4, 2, 16, block.shape[1])
    ordered[pl.ds(4 * q, 4)] = block[:128].reshape(shape)
    ordered[pl.ds(16 + 4 * q, 4)] = block[128:].reshape(shape)


def ascent_kernel(at, gram, gram_other, p0, p1, p2, p3, c0, c1, c2, c3, mark, slopes, along_far, ordered, pres, cots, along, sems):
    core, x = at[1], at[2]
    sources = (p0, c0, p1, c1, p2, c2, p3, c3)
    targets = [v.at[b] for b in range(4) for v in (pres, cots)]
    copies = fetch(sources, targets, sems)
    columns = along.shape[1]
    for b in range(4):
        copies[2 * b].wait()
        copies[2 * b + 1].wait()
        slope = slope_of(cots[b].reshape(256, columns), pres[b].astype(F32))
        slopes[b] = slope
        put(x ^ b, slope, ordered)
    half = TOKENS // 2
    part = jnp.zeros((256, columns), F32)
    for source, c in ((gram, core), (gram_other, 1 - core)):
        right = ordered[:, c].reshape(half, columns)
        for i in range(2):
            part = part + dot(source[:, i].reshape(half, 256), right, ((0,), (0,)))
    along[...] = part.astype(BF)
    fetch((along,), (along_far,), sems.at[pl.ds(8, 1)])[0].wait()


def ascent_work(at, gram, gram_other, pres, cots, mark):
    columns = pres[0].shape[1]
    vmem = pl.BlockSpec(memory_space=pltpu.VMEM)
    return pl.pallas_call(
        ascent_kernel,
        out_shape=[jax.ShapeDtypeStruct((4, 256, columns), BF), jax.ShapeDtypeStruct((256, columns), BF)],
        in_specs=[pl.BlockSpec(memory_space=pltpu.SMEM), vmem, vmem] + [HBM] * 9,
        out_specs=[vmem, HBM],
        scratch_shapes=[
            pltpu.VMEM((32, 2, 16, columns), BF),
            pltpu.VMEM((4, 256, columns), BF),
            pltpu.VMEM((4, 2, 128, columns), BF),
            pltpu.VMEM((256, columns), BF),
            pltpu.SemaphoreType.DMA((9,)),
        ],
        compiler_params=pltpu.CompilerParams(vmem_limit_bytes=40 << 20),
        cost_estimate=pl.CostEstimate(flops=2 * TOKENS * 256 * columns, bytes_accessed=3 << 20, transcendentals=2 * TOKENS * columns),
        name="ascent_work",
    )(at, gram, gram_other, *pres, *cots, mark)


def sum_kernel(slopes, a0, a1, a2, a3, squared, alongs, sems):
    total = jnp.zeros((1, alongs.shape[2]), F32)
    for b, copy in enumerate(fetch((a0, a1, a2, a3), [alongs.at[b] for b in range(4)], sems)):
        copy.wait()
        total = total + jnp.sum(alongs[b].astype(F32) * slopes[b].astype(F32), axis=0, keepdims=True)
    total = jnp.sum(total, axis=1, keepdims=True)
    squared[...] = jnp.broadcast_to(total.reshape(1, 1, 1), squared.shape)


def sum_work(slopes, alongs):
    vmem = pl.BlockSpec(memory_space=pltpu.VMEM)
    return pl.pallas_call(
        sum_kernel,
        out_shape=jax.ShapeDtypeStruct((64, 1, 128), F32),
        in_specs=[vmem] + [HBM] * 4,
        out_specs=vmem,
        scratch_shapes=[pltpu.VMEM(slopes.shape, BF), pltpu.SemaphoreType.DMA((4,))],
        compiler_params=pltpu.CompilerParams(vmem_limit_bytes=40 << 20),
        cost_estimate=pl.CostEstimate(flops=1 << 20, bytes_accessed=2 << 20, transcendentals=0),
        name="sum_work",
    )(slopes, *alongs)


def result_kernel(at, got, turned, p0, p1, p2, p3, c0, c1, c2, c3, a0, a1, a2, a3, out, ordered, pres, cots, alongs, sems):
    x = at[2]
    sources = (p0, c0, a0, p1, c1, a1, p2, c2, a2, p3, c3, a3)
    targets = [v.at[b] for b in range(4) for v in (pres, cots, alongs)]
    copies = fetch(sources, targets, sems)
    columns = out.shape[1]
    squared = jnp.sum(got[...].reshape(64, 128), axis=0, keepdims=True)[:, :1]
    step = 0.5 * math.sqrt(FF) / (jnp.sqrt(jnp.maximum(squared, 0.0)) + 1e-12)
    for b in range(4):
        for copy in copies[3 * b : 3 * b + 3]:
            copy.wait()
        value = pres[b].astype(F32) + alongs[b].astype(F32) * step
        put(x ^ b, slope_of(cots[b].reshape(256, columns), value), ordered)
    out[...] = dot(turned[...], ordered[...].reshape(TOKENS, columns), ((1,), (0,)))


def result_work(at, got, turned, pres, cots, alongs):
    columns = pres[0].shape[1]
    vmem = pl.BlockSpec(memory_space=pltpu.VMEM)
    return pl.pallas_call(
        result_kernel,
        out_shape=jax.ShapeDtypeStruct((turned.shape[0], columns), F32),
        in_specs=[pl.BlockSpec(memory_space=pltpu.SMEM), vmem, vmem] + [HBM] * 12,
        out_specs=vmem,
        scratch_shapes=[
            pltpu.VMEM((32, 2, 16, columns), BF),
            pltpu.VMEM((4, 256, columns), BF),
            pltpu.VMEM((4, 2, 128, columns), BF),
            pltpu.VMEM((4, 256, columns), BF),
            pltpu.SemaphoreType.DMA((12,)),
        ],
        compiler_params=pltpu.CompilerParams(vmem_limit_bytes=40 << 20),
        cost_estimate=pl.CostEstimate(flops=2 * TOKENS * 768 * columns, bytes_accessed=4 << 20, transcendentals=2 * TOKENS * columns),
        name="result_work",
    )(at, got, turned, *pres, *cots, *alongs)


def per_device(tokens, norm_gain, w_up, cotangent):
    width = w_up.shape[0]
    places = (lax.axis_index(DP), lax.axis_index("c"), lax.axis_index("x"), lax.axis_index("yh"))
    at = jnp.stack(places).astype(jnp.int32)
    with jax.named_scope("token_gather"):
        mine = spread(tokens, ("yl", "z"), 32)
        mine, late = lax.optimization_barrier((mine, cotangent))
        other = swap(mine, "c", 1)
        cot_other = swap(late, "yh", 1)
    with jax.named_scope("local_work"):
        joined, own, near, opposite, far, sent = local_work(at, mine, other, norm_gain[None], w_up)
    with jax.named_scope("sums_x"):
        sent, cot_other = lax.optimization_barrier((sent, cot_other))
        got = lax.all_to_all(sent, MP, 0, 0, tiled=True)
        moved = [swap(v, "x", b) for b, v in ((1, near), (2, opposite), (3, far))]
    with jax.named_scope("stats_work"):
        rows, half, full, pair, scales = stats_work(at, got, own, moved, cotangent, cot_other)
        turned = norm_work(joined, scales, norm_gain[None])
    with jax.named_scope("gram_gather"):
        gram = spread(rows, ("yl", "z"), 32)
    with jax.named_scope("pre"):
        moved = swap(half, "yh", 1)
        cots = gather_x(pair)
        pre, mark = pre_work(at, full, moved, scales, turned, cots[1:])
        gram, mark = lax.optimization_barrier((gram, mark))
        gram_other = swap(gram, "c", 1)
        pres = gather_x(pre)
    with jax.named_scope("ascent"):
        slopes, along = ascent_work(at, gram, gram_other, pres, cots, mark)
        alongs = gather_x(along)
        squared = sum_work(slopes, alongs)
        squared = lax.all_to_all(squared, DP, 0, 0, tiled=True)
    with jax.named_scope("sharp"):
        return result_work(at, squared, turned, pres, cots, alongs)


def solution(mesh):
    fine = Mesh(mesh.devices.reshape(4, 8, 2, 2, 4), DP + MP)
    placed = (P(DP, MP), P(MP), P(MP, DP), P(MP, DP))
    return jax.shard_map(
        per_device, mesh=fine, in_specs=placed, out_specs=P(MP, DP), check_vma=False
    )
```

```python
import math

import jax
import jax.numpy as jnp
from jax import lax
from jax.experimental import pallas as pl
from jax.experimental.pallas import tpu as pltpu
from jax.sharding import Mesh
from jax.sharding import PartitionSpec as P

FF = 24576
D = 6144
TOKENS = 1024
DP = ("yl", "z", "c")
MP = ("yh", "x")
BF = jnp.bfloat16
F32 = jnp.float32


def gelu_slope(value):
    cdf = 0.5 * (1.0 + lax.erf(value * (1.0 / math.sqrt(2.0))))
    dens = jnp.exp(-0.5 * value * value) * (1.0 / math.sqrt(2.0 * math.pi))
    return cdf + value * dens


def swap(value, axis, bit):
    size = lax.axis_size(axis)
    return lax.ppermute(value, axis, [(i, i ^ bit) for i in range(size)])


def spread(value, axes, count):
    copies = jnp.broadcast_to(value[None], (count,) + value.shape)
    return lax.all_to_all(copies, axes, 0, 0, tiled=True)


def gather_x(value):
    return [value] + [swap(value, "x", b) for b in (1, 2, 3)]


def dot(left, right, dims, precision=None):
    return lax.dot_general(left, right, (dims, ((), ())), precision=precision, preferred_element_type=F32)


def split(value, count):
    out = []
    for _ in range(count):
        out.append(value.astype(BF).astype(F32))
        value = value - out[-1]
    return out


def local_kernel(at, mine, other, gain, w, joined, own, near, opposite, far, sent, high, part, out, sems):
    place, core, x = at[0], at[1], at[2]
    g = gain[...]
    width = g.shape[1]
    ones = jnp.ones((8, width), BF)
    gains = jnp.concatenate(split(g, 3) + [jnp.zeros((5, width), F32)], axis=0).astype(BF)
    local, css, lean = [], [], []
    for i in range(8):
        chips = pl.ds(4 * i, 4)
        joined[chips, core] = mine[chips]
        joined[chips, 1 - core] = other[chips]
        raw = joined[chips].reshape(128, width)
        value = raw.astype(F32)
        centred = value - jnp.sum(value, axis=1, keepdims=True) * (1.0 / width)
        full = centred * g
        first = full.astype(BF)
        second = (full - first.astype(F32)).astype(BF)
        high[pl.ds(128 * i, 128)] = first
        rows = dot(first, w[...], ((1,), (0,))) + dot(second, w[...], ((1,), (0,)))
        part[i // 2, pl.ds(128 * (i % 2), 128)] = rows
        square = centred * centred
        top = square.astype(BF)
        rest = (square - top.astype(F32)).astype(BF)
        across = ((1,), (1,))
        local.append(dot(ones, raw, across)[:1] * (1.0 / width))
        css.append((dot(ones, top, across) + dot(ones, rest, across))[:1])
        lean.append(jnp.sum(dot(gains, first, across), axis=0, keepdims=True))
    own[...] = part[x]
    copies = []
    for b, target in ((1, near), (2, opposite), (3, far)):
        out[b - 1] = part[x ^ b].astype(BF)
        copies.append(pltpu.make_async_copy(out.at[b - 1], target, sems.at[b - 1]))
        copies[-1].start()
    gram = dot(high[pl.ds(pl.multiple_of(place * 16, 16), 16)], high[...], ((1,), (1,)))
    local, css, lean = (jnp.concatenate(v, axis=1) for v in (local, css, lean))
    column = jnp.sum(dot(gains, w[...], ((1,), (0,))), axis=0, keepdims=True)
    power = jnp.broadcast_to(jnp.sum(g * g, axis=1, keepdims=True), (1, 128))
    extra = jnp.concatenate(split(column, 2) + split(power, 2), axis=1)
    rows = split(gram, 2) + split(local, 3) + split(css, 2) + split(lean, 2) + [extra]
    sent[...] = jnp.concatenate(rows, axis=0).astype(BF)
    for copy in copies:
        copy.wait()


def local_work(at, mine, other, gain, w):
    width, columns = w.shape
    block = jax.ShapeDtypeStruct((256, columns), BF)
    vmem = pl.BlockSpec(memory_space=pltpu.VMEM)
    return pl.pallas_call(
        local_kernel,
        out_shape=[
            jax.ShapeDtypeStruct((32, 2, 16, width), BF),
            jax.ShapeDtypeStruct((256, columns), F32),
            block,
            block,
            block,
            jax.ShapeDtypeStruct((40, TOKENS), BF),
        ],
        in_specs=[pl.BlockSpec(memory_space=pltpu.SMEM)] + [vmem] * 4,
        out_specs=[vmem] * 2 + [pl.BlockSpec(memory_space=pl.ANY)] * 3 + [vmem],
        scratch_shapes=[
            pltpu.VMEM((TOKENS, width), BF),
            pltpu.VMEM((4, 256, columns), F32),
            pltpu.VMEM((3, 256, columns), BF),
            pltpu.SemaphoreType.DMA((3,)),
        ],
        compiler_params=pltpu.CompilerParams(vmem_limit_bytes=40 << 20),
        cost_estimate=pl.CostEstimate(flops=2 * TOKENS * width * columns * 2, bytes_accessed=8 << 20, transcendentals=0),
        name="local_work",
    )(at, mine, other, gain, w)


def stats_kernel(at, got, own, one, two, three, cot, cot_other, rows, half, full, pair, scales, turned):
    place, x, low = at[0], at[2], at[3] == 0
    exact = lax.Precision.HIGHEST
    columns = own.shape[1]
    total = own[...] + one[...].astype(F32) + two[...].astype(F32) + three[...].astype(F32)
    half[...] = total.astype(BF)
    pair[at[3]] = cot[...]
    pair[1 - at[3]] = cot_other[...]
    gram = jnp.zeros((16, TOKENS), F32)
    for j in range(8):
        gram = gram + (got[j, :16].astype(F32) + got[j, 16:32].astype(F32))
    terms = [got[j, 32:40].astype(F32) for j in range(8)]
    local = jnp.concatenate([t[0:1] + t[1:2] + t[2:3] for t in terms], axis=0)
    css = jnp.concatenate([t[3:4] + t[4:5] for t in terms], axis=0)
    lean = jnp.concatenate([t[5:6] + t[6:7] for t in terms], axis=0)
    column = jnp.concatenate([t[7:8, :columns] + t[7:8, columns : 2 * columns] for t in terms], axis=0)
    power = jnp.concatenate([t[7:8, 2 * columns : 2 * columns + 1] + t[7:8, 2 * columns + 128 : 2 * columns + 129] for t in terms], axis=0)
    mean = jnp.sum(local, axis=0, keepdims=True) / 8
    apart = local - mean
    var = (jnp.sum(css, axis=0, keepdims=True) + (D // 8) * jnp.sum(apart * apart, axis=0, keepdims=True)) / D
    inv = lax.rsqrt(var + 1e-06)
    flat = jnp.concatenate([lean, apart, power * apart, apart, inv, mean, jnp.zeros((94, TOKENS), F32)], axis=0)
    turned[...] = flat.T
    mine = turned[pl.ds(pl.multiple_of(place * 16, 16), 16)]
    right = jnp.concatenate([apart, lean, apart], axis=0)
    gram = (gram + dot(mine[:, :24], right, ((1,), (0,)), exact)) * mine[:, 32:33] * inv
    rows[...] = gram.astype(BF)
    here = turned[pl.ds(pl.multiple_of(x * 256, 256), 256)]
    full[...] = total + dot(here[:, 24:32], column, ((1,), (0,)), exact)
    scales[...] = turned[...]


def stats_work(at, got, own, moved, cot, cot_other):
    columns = own.shape[1]
    vmem = pl.BlockSpec(memory_space=pltpu.VMEM)
    return pl.pallas_call(
        stats_kernel,
        out_shape=[
            jax.ShapeDtypeStruct((16, TOKENS), BF),
            jax.ShapeDtypeStruct((256, columns), BF),
            jax.ShapeDtypeStruct((256, columns), F32),
            jax.ShapeDtypeStruct((2, 128, columns), BF),
            jax.ShapeDtypeStruct((TOKENS, 128), F32),
        ],
        in_specs=[pl.BlockSpec(memory_space=pltpu.SMEM)] + [vmem] * 7,
        out_specs=[vmem] * 5,
        scratch_shapes=[pltpu.VMEM((TOKENS, 128), F32)],
        compiler_params=pltpu.CompilerParams(vmem_limit_bytes=40 << 20),
        cost_estimate=pl.CostEstimate(flops=10 << 20, bytes_accessed=3 << 20, transcendentals=0),
        name="stats_work",
    )(at, got, own, *moved, cot, cot_other)


def pre_kernel(at, full, moved, scales, one, two, three, out, mark):
    inv = scales[pl.ds(pl.multiple_of(at[2] * 256, 256), 256)][:, 32:33]
    out[...] = ((full[...] + moved[...].astype(F32)) * inv).astype(BF)
    mark[...] = inv[:8]


def pre_work(at, full, moved, scales, cots):
    vmem = pl.BlockSpec(memory_space=pltpu.VMEM)
    return pl.pallas_call(
        pre_kernel,
        out_shape=[jax.ShapeDtypeStruct(full.shape, BF), jax.ShapeDtypeStruct((8, 1), F32)],
        in_specs=[pl.BlockSpec(memory_space=pltpu.SMEM)] + [vmem] * 3 + [pl.BlockSpec(memory_space=pl.ANY)] * 3,
        out_specs=[vmem] * 2,
        compiler_params=pltpu.CompilerParams(vmem_limit_bytes=40 << 20),
        cost_estimate=pl.CostEstimate(flops=1 << 20, bytes_accessed=1 << 20, transcendentals=0),
        name="pre_work",
    )(at, full, moved, scales, *cots)


def slope_of(cot, value):
    return (cot.astype(F32) * gelu_slope(value) * (1.0 / math.sqrt(TOKENS))).astype(BF)


def ascent_kernel(at, mine, other, p0, p1, p2, p3, c0, c1, c2, c3, mark, along, pre_out, cot_out, squared, slope, pre, cot, sems):
    core, x = at[1], at[2]
    columns = p0.shape[1]
    for b, (p, c) in enumerate(((p0, c0), (p1, c1), (p2, c2), (p3, c3))):
        q = x ^ b
        pre[pl.ds(pl.multiple_of(q * 256, 256), 256)] = p[...]
        cot[pl.ds(pl.multiple_of(q * 128, 128), 128)] = c[0]
        cot[pl.ds(pl.multiple_of(512 + q * 128, 128), 128)] = c[1]
    copies = [pltpu.make_async_copy(pre, pre_out, sems.at[0]), pltpu.make_async_copy(cot, cot_out, sems.at[1])]
    for copy in copies:
        copy.start()
    for i in range(8):
        rows = pl.ds(128 * i, 128)
        value = slope_of(cot[rows], pre[rows].astype(F32))
        slope[pl.ds(4 * i, 4)] = value.reshape(4, 2, 16, columns)
    total = jnp.zeros((1, 1), F32)
    for gram, c in ((mine, core), (other, 1 - core)):
        for i in range(2):
            chips = pl.ds(16 * i, 16)
            part = dot(gram[chips].reshape(256, TOKENS), slope[...].reshape(TOKENS, columns), ((1,), (0,)))
            along[chips, c] = part.reshape(16, 16, columns)
            weighed = part * slope[chips, c].reshape(256, columns).astype(F32)
            total = total + jnp.sum(jnp.sum(weighed, axis=0, keepdims=True), axis=1, keepdims=True)
    squared[...] = jnp.broadcast_to(total.reshape(1, 1, 1), squared.shape)
    for copy in copies:
        copy.wait()


def ascent_work(at, mine, other, pres, cots, mark):
    columns = pres[0].shape[1]
    vmem = pl.BlockSpec(memory_space=pltpu.VMEM)
    anywhere = pl.BlockSpec(memory_space=pl.ANY)
    flat = jax.ShapeDtypeStruct((TOKENS, columns), BF)
    return pl.pallas_call(
        ascent_kernel,
        out_shape=[
            jax.ShapeDtypeStruct((32, 2, 16, columns), F32),
            flat,
            flat,
            jax.ShapeDtypeStruct((64, 1, 128), F32),
        ],
        in_specs=[pl.BlockSpec(memory_space=pltpu.SMEM)] + [vmem] * 10 + [anywhere],
        out_specs=[vmem, anywhere, anywhere, vmem],
        scratch_shapes=[
            pltpu.VMEM((32, 2, 16, columns), BF),
            pltpu.VMEM((TOKENS, columns), BF),
            pltpu.VMEM((TOKENS, columns), BF),
            pltpu.SemaphoreType.DMA((2,)),
        ],
        compiler_params=pltpu.CompilerParams(vmem_limit_bytes=40 << 20),
        cost_estimate=pl.CostEstimate(flops=2 * TOKENS * TOKENS * columns, bytes_accessed=8 << 20, transcendentals=2 * TOKENS * columns),
        name="ascent_work",
    )(at, mine, other, *pres, *cots, mark)


def per_device(tokens, norm_gain, w_up, cotangent):
    width, columns = w_up.shape
    places = (lax.axis_index(DP), lax.axis_index("c"), lax.axis_index("x"), lax.axis_index("yh"))
    at = jnp.stack(places).astype(jnp.int32)
    with jax.named_scope("token_gather"):
        mine = spread(tokens, ("yl", "z"), 32)
        mine, late = lax.optimization_barrier((mine, cotangent))
        other = swap(mine, "c", 1)
        cot_other = swap(late, "yh", 1)
    with jax.named_scope("local_work"):
        joined, own, near, opposite, far, sent = local_work(at, mine, other, norm_gain[None], w_up)
    with jax.named_scope("sums_x"):
        sent, cot_other = lax.optimization_barrier((sent, cot_other))
        got = spread(sent, MP, 8)
        moved = [swap(v, "x", b) for b, v in ((1, near), (2, opposite), (3, far))]
    with jax.named_scope("stats_work"):
        rows, half, full, pair, scales = stats_work(at, got, own, moved, cotangent, cot_other)
        normed = joined.reshape(TOKENS, width).astype(F32) - scales[:, 33:34]
        normed = (normed * scales[:, 32:33] * norm_gain[None, :]).astype(BF)
    with jax.named_scope("gram_gather"):
        gram = spread(rows, ("yl", "z"), 32)
    with jax.named_scope("pre"):
        moved = swap(half, "yh", 1)
        cots = gather_x(pair)
        pre, mark = pre_work(at, full, moved, scales, cots[1:])
        gram, mark = lax.optimization_barrier((gram, mark))
        pres = gather_x(pre)
        gram_other = swap(gram, "c", 1)
    with jax.named_scope("ascent"):
        along, pre, cot, squared = ascent_work(at, gram, gram_other, pres, cots, mark)
        squared = jnp.sum(lax.all_to_all(squared, DP, 0, 0, tiled=True)[:, 0, 0])
        size = jnp.sqrt(jnp.maximum(squared, 0.0)) + 1e-12
        radius = 0.5 * math.sqrt(FF)
    with jax.named_scope("sharp"):
        sharp = slope_of(cot, pre.astype(F32) + along.reshape(TOKENS, columns) * (radius / size))
        return dot(normed, sharp, ((0,), (0,)))


def solution(mesh):
    fine = Mesh(mesh.devices.reshape(4, 8, 2, 2, 4), DP + MP)
    placed = (P(DP, MP), P(MP), P(MP, DP), P(MP, DP))
    return jax.shard_map(
        per_device, mesh=fine, in_specs=placed, out_specs=P(MP, DP), check_vma=False
    )
```

```python
import math

import jax
import jax.numpy as jnp
from jax import lax
from jax.experimental import pallas as pl
from jax.experimental.pallas import tpu as pltpu
from jax.sharding import Mesh
from jax.sharding import PartitionSpec as P

FF = 24576
D = 6144
TOKENS = 1024
DP = ("yl", "z", "c")
MP = ("yh", "x")
BF = jnp.bfloat16
F32 = jnp.float32


def gelu_slope(value):
    cdf = 0.5 * (1.0 + lax.erf(value * (1.0 / math.sqrt(2.0))))
    dens = jnp.exp(-0.5 * value * value) * (1.0 / math.sqrt(2.0 * math.pi))
    return cdf + value * dens


def swap(value, axis, bit):
    size = lax.axis_size(axis)
    return lax.ppermute(value, axis, [(i, i ^ bit) for i in range(size)])


def spread(value, axes, count):
    copies = jnp.broadcast_to(value[None], (count,) + value.shape)
    return lax.all_to_all(copies, axes, 0, 0, tiled=True)


def gather_x(value):
    return [value] + [swap(value, "x", b) for b in (1, 2, 3)]


def dot(left, right, dims, precision=None):
    return lax.dot_general(left, right, (dims, ((), ())), precision=precision, preferred_element_type=F32)


def split(value, count):
    out = []
    for _ in range(count):
        out.append(value.astype(BF).astype(F32))
        value = value - out[-1]
    return out


def local_kernel(at, mine, other, gain, w, joined, own, near, opposite, far, sent, high, part, out, sems):
    place, core, x = at[0], at[1], at[2]
    g = gain[...]
    width = g.shape[1]
    ones = jnp.ones((8, width), BF)
    gains = jnp.concatenate(split(g, 3) + [jnp.zeros((5, width), F32)], axis=0).astype(BF)
    local, css, lean = [], [], []
    for i in range(8):
        chips = pl.ds(4 * i, 4)
        joined[chips, core] = mine[chips]
        joined[chips, 1 - core] = other[chips]
        raw = joined[chips].reshape(128, width)
        value = raw.astype(F32)
        centred = value - jnp.sum(value, axis=1, keepdims=True) * (1.0 / width)
        full = centred * g
        first = full.astype(BF)
        second = (full - first.astype(F32)).astype(BF)
        high[pl.ds(128 * i, 128)] = first
        rows = dot(first, w[...], ((1,), (0,))) + dot(second, w[...], ((1,), (0,)))
        part[i // 2, pl.ds(128 * (i % 2), 128)] = rows
        square = centred * centred
        top = square.astype(BF)
        rest = (square - top.astype(F32)).astype(BF)
        across = ((1,), (1,))
        local.append(dot(ones, raw, across)[:1] * (1.0 / width))
        css.append((dot(ones, top, across) + dot(ones, rest, across))[:1])
        lean.append(jnp.sum(dot(gains, first, across), axis=0, keepdims=True))
    own[...] = part[x]
    copies = []
    for b, target in ((1, near), (2, opposite), (3, far)):
        out[b - 1] = part[x ^ b].astype(BF)
        copies.append(pltpu.make_async_copy(out.at[b - 1], target, sems.at[b - 1]))
        copies[-1].start()
    gram = dot(high[pl.ds(pl.multiple_of(place * 16, 16), 16)], high[...], ((1,), (1,)))
    local, css, lean = (jnp.concatenate(v, axis=1) for v in (local, css, lean))
    column = jnp.sum(dot(gains, w[...], ((1,), (0,))), axis=0, keepdims=True)
    power = jnp.broadcast_to(jnp.sum(g * g, axis=1, keepdims=True), (1, 128))
    extra = jnp.concatenate(split(column, 2) + split(power, 2), axis=1)
    rows = split(gram, 2) + split(local, 3) + split(css, 2) + split(lean, 2) + [extra]
    sent[...] = jnp.concatenate(rows, axis=0).astype(BF)
    for copy in copies:
        copy.wait()


def local_work(at, mine, other, gain, w):
    width, columns = w.shape
    block = jax.ShapeDtypeStruct((256, columns), BF)
    vmem = pl.BlockSpec(memory_space=pltpu.VMEM)
    return pl.pallas_call(
        local_kernel,
        out_shape=[
            jax.ShapeDtypeStruct((32, 2, 16, width), BF),
            jax.ShapeDtypeStruct((256, columns), F32),
            block,
            block,
            block,
            jax.ShapeDtypeStruct((40, TOKENS), BF),
        ],
        in_specs=[pl.BlockSpec(memory_space=pltpu.SMEM)] + [vmem] * 4,
        out_specs=[vmem] * 2 + [pl.BlockSpec(memory_space=pl.ANY)] * 3 + [vmem],
        scratch_shapes=[
            pltpu.VMEM((TOKENS, width), BF),
            pltpu.VMEM((4, 256, columns), F32),
            pltpu.VMEM((3, 256, columns), BF),
            pltpu.SemaphoreType.DMA((3,)),
        ],
        compiler_params=pltpu.CompilerParams(vmem_limit_bytes=40 << 20),
        cost_estimate=pl.CostEstimate(flops=2 * TOKENS * width * columns * 2, bytes_accessed=8 << 20, transcendentals=0),
        name="local_work",
    )(at, mine, other, gain, w)


def stats_kernel(at, got, own, one, two, three, cot, cot_other, rows, half, full, pair, scales, turned):
    place, x, low = at[0], at[2], at[3] == 0
    exact = lax.Precision.HIGHEST
    columns = own.shape[1]
    total = own[...] + one[...].astype(F32) + two[...].astype(F32) + three[...].astype(F32)
    half[...] = total.astype(BF)
    pair[at[3]] = cot[...]
    pair[1 - at[3]] = cot_other[...]
    gram = jnp.zeros((16, TOKENS), F32)
    for j in range(8):
        gram = gram + (got[j, :16].astype(F32) + got[j, 16:32].astype(F32))
    terms = [got[j, 32:40].astype(F32) for j in range(8)]
    local = jnp.concatenate([t[0:1] + t[1:2] + t[2:3] for t in terms], axis=0)
    css = jnp.concatenate([t[3:4] + t[4:5] for t in terms], axis=0)
    lean = jnp.concatenate([t[5:6] + t[6:7] for t in terms], axis=0)
    column = jnp.concatenate([t[7:8, :columns] + t[7:8, columns : 2 * columns] for t in terms], axis=0)
    power = jnp.concatenate([t[7:8, 2 * columns : 2 * columns + 1] + t[7:8, 2 * columns + 128 : 2 * columns + 129] for t in terms], axis=0)
    mean = jnp.sum(local, axis=0, keepdims=True) / 8
    apart = local - mean
    var = (jnp.sum(css, axis=0, keepdims=True) + (D // 8) * jnp.sum(apart * apart, axis=0, keepdims=True)) / D
    inv = lax.rsqrt(var + 1e-06)
    flat = jnp.concatenate([lean, apart, power * apart, apart, inv, mean, jnp.zeros((94, TOKENS), F32)], axis=0)
    turned[...] = flat.T
    mine = turned[pl.ds(pl.multiple_of(place * 16, 16), 16)]
    right = jnp.concatenate([apart, lean, apart], axis=0)
    gram = (gram + dot(mine[:, :24], right, ((1,), (0,)), exact)) * mine[:, 32:33] * inv
    rows[...] = gram.astype(BF)
    here = turned[pl.ds(pl.multiple_of(x * 256, 256), 256)]
    full[...] = total + dot(here[:, 24:32], column, ((1,), (0,)), exact)
    scales[...] = turned[...]


def stats_work(at, got, own, moved, cot, cot_other):
    columns = own.shape[1]
    vmem = pl.BlockSpec(memory_space=pltpu.VMEM)
    return pl.pallas_call(
        stats_kernel,
        out_shape=[
            jax.ShapeDtypeStruct((16, TOKENS), BF),
            jax.ShapeDtypeStruct((256, columns), BF),
            jax.ShapeDtypeStruct((256, columns), F32),
            jax.ShapeDtypeStruct((2, 128, columns), BF),
            jax.ShapeDtypeStruct((TOKENS, 128), F32),
        ],
        in_specs=[pl.BlockSpec(memory_space=pltpu.SMEM)] + [vmem] * 7,
        out_specs=[vmem] * 5,
        scratch_shapes=[pltpu.VMEM((TOKENS, 128), F32)],
        compiler_params=pltpu.CompilerParams(vmem_limit_bytes=40 << 20),
        cost_estimate=pl.CostEstimate(flops=10 << 20, bytes_accessed=3 << 20, transcendentals=0),
        name="stats_work",
    )(at, got, own, *moved, cot, cot_other)


def pre_kernel(at, full, moved, scales, one, two, three, out, mark):
    inv = scales[pl.ds(pl.multiple_of(at[2] * 256, 256), 256)][:, 32:33]
    out[...] = ((full[...] + moved[...].astype(F32)) * inv).astype(BF)
    mark[...] = inv[:8]


def pre_work(at, full, moved, scales, cots):
    vmem = pl.BlockSpec(memory_space=pltpu.VMEM)
    return pl.pallas_call(
        pre_kernel,
        out_shape=[jax.ShapeDtypeStruct(full.shape, BF), jax.ShapeDtypeStruct((8, 1), F32)],
        in_specs=[pl.BlockSpec(memory_space=pltpu.SMEM)] + [vmem] * 3 + [pl.BlockSpec(memory_space=pl.ANY)] * 3,
        out_specs=[vmem] * 2,
        compiler_params=pltpu.CompilerParams(vmem_limit_bytes=40 << 20),
        cost_estimate=pl.CostEstimate(flops=1 << 20, bytes_accessed=1 << 20, transcendentals=0),
        name="pre_work",
    )(at, full, moved, scales, *cots)


def slope_of(cot, value):
    return (cot.astype(F32) * gelu_slope(value) * (1.0 / math.sqrt(TOKENS))).astype(BF)


def ascent_kernel(at, mine, other, p0, p1, p2, p3, c0, c1, c2, c3, mark, along, pre_out, cot_out, squared, slope, pre, cot, sems):
    core, x = at[1], at[2]
    columns = p0.shape[1]
    arrivals = []
    for b, (p, c) in enumerate(((p0, c0), (p1, c1), (p2, c2), (p3, c3))):
        q = x ^ b
        places = (
            (p, pre.at[pl.ds(pl.multiple_of(q * 256, 256), 256)]),
            (c.at[0], cot.at[pl.ds(pl.multiple_of(q * 128, 128), 128)]),
            (c.at[1], cot.at[pl.ds(pl.multiple_of(512 + q * 128, 128), 128)]),
        )
        for i, (source, target) in enumerate(places):
            arrivals.append(pltpu.make_async_copy(source, target, sems.at[2 + 3 * b + i]))
            arrivals[-1].start()
    for copy in arrivals:
        copy.wait()
    copies = [pltpu.make_async_copy(pre, pre_out, sems.at[0]), pltpu.make_async_copy(cot, cot_out, sems.at[1])]
    for copy in copies:
        copy.start()
    for i in range(8):
        rows = pl.ds(128 * i, 128)
        value = slope_of(cot[rows], pre[rows].astype(F32))
        slope[pl.ds(4 * i, 4)] = value.reshape(4, 2, 16, columns)
    total = jnp.zeros((1, 1), F32)
    for gram, c in ((mine, core), (other, 1 - core)):
        for i in range(2):
            chips = pl.ds(16 * i, 16)
            part = dot(gram[chips].reshape(256, TOKENS), slope[...].reshape(TOKENS, columns), ((1,), (0,)))
            along[chips, c] = part.reshape(16, 16, columns)
            weighed = part * slope[chips, c].reshape(256, columns).astype(F32)
            total = total + jnp.sum(jnp.sum(weighed, axis=0, keepdims=True), axis=1, keepdims=True)
    squared[...] = jnp.broadcast_to(total.reshape(1, 1, 1), squared.shape)
    for copy in copies:
        copy.wait()


def ascent_work(at, mine, other, pres, cots, mark):
    columns = pres[0].shape[1]
    vmem = pl.BlockSpec(memory_space=pltpu.VMEM)
    anywhere = pl.BlockSpec(memory_space=pl.ANY)
    far = pl.BlockSpec(memory_space=pltpu.HBM)
    flat = jax.ShapeDtypeStruct((TOKENS, columns), BF)
    return pl.pallas_call(
        ascent_kernel,
        out_shape=[
            jax.ShapeDtypeStruct((32, 2, 16, columns), F32),
            flat,
            flat,
            jax.ShapeDtypeStruct((64, 1, 128), F32),
        ],
        in_specs=[pl.BlockSpec(memory_space=pltpu.SMEM)] + [vmem] * 2 + [far] * 8 + [anywhere],
        out_specs=[vmem, far, far, vmem],
        scratch_shapes=[
            pltpu.VMEM((32, 2, 16, columns), BF),
            pltpu.VMEM((TOKENS, columns), BF),
            pltpu.VMEM((TOKENS, columns), BF),
            pltpu.SemaphoreType.DMA((14,)),
        ],
        compiler_params=pltpu.CompilerParams(vmem_limit_bytes=40 << 20),
        cost_estimate=pl.CostEstimate(flops=2 * TOKENS * TOKENS * columns, bytes_accessed=8 << 20, transcendentals=2 * TOKENS * columns),
        name="ascent_work",
    )(at, mine, other, *pres, *cots, mark)


def per_device(tokens, norm_gain, w_up, cotangent):
    width, columns = w_up.shape
    places = (lax.axis_index(DP), lax.axis_index("c"), lax.axis_index("x"), lax.axis_index("yh"))
    at = jnp.stack(places).astype(jnp.int32)
    with jax.named_scope("token_gather"):
        mine = spread(tokens, ("yl", "z"), 32)
        mine, late = lax.optimization_barrier((mine, cotangent))
        other = swap(mine, "c", 1)
        cot_other = swap(late, "yh", 1)
    with jax.named_scope("local_work"):
        joined, own, near, opposite, far, sent = local_work(at, mine, other, norm_gain[None], w_up)
    with jax.named_scope("sums_x"):
        sent, cot_other = lax.optimization_barrier((sent, cot_other))
        got = spread(sent, MP, 8)
        moved = [swap(v, "x", b) for b, v in ((1, near), (2, opposite), (3, far))]
    with jax.named_scope("stats_work"):
        rows, half, full, pair, scales = stats_work(at, got, own, moved, cotangent, cot_other)
        normed = joined.reshape(TOKENS, width).astype(F32) - scales[:, 33:34]
        normed = (normed * scales[:, 32:33] * norm_gain[None, :]).astype(BF)
    with jax.named_scope("gram_gather"):
        gram = spread(rows, ("yl", "z"), 32)
    with jax.named_scope("pre"):
        moved = swap(half, "yh", 1)
        cots = gather_x(pair)
        pre, mark = pre_work(at, full, moved, scales, cots[1:])
        gram, mark = lax.optimization_barrier((gram, mark))
        pres = gather_x(pre)
        gram_other = swap(gram, "c", 1)
    with jax.named_scope("ascent"):
        along, pre, cot, squared = ascent_work(at, gram, gram_other, pres, cots, mark)
        squared = jnp.sum(lax.all_to_all(squared, DP, 0, 0, tiled=True)[:, 0, 0])
        size = jnp.sqrt(jnp.maximum(squared, 0.0)) + 1e-12
        radius = 0.5 * math.sqrt(FF)
    with jax.named_scope("sharp"):
        sharp = slope_of(cot, pre.astype(F32) + along.reshape(TOKENS, columns) * (radius / size))
        return dot(normed, sharp, ((0,), (0,)))


def solution(mesh):
    fine = Mesh(mesh.devices.reshape(4, 8, 2, 2, 4), DP + MP)
    placed = (P(DP, MP), P(MP), P(MP, DP), P(MP, DP))
    return jax.shard_map(
        per_device, mesh=fine, in_specs=placed, out_specs=P(MP, DP), check_vma=False
    )
```
